512 devices in a mesh: lat: 64 (over z, y), chan: 2 (over core), obs: 4 (over x).
Axes of the slice: x: 4, y: 8, z: 8, core: 2. Of those that a mesh axis runs over, the one named last changes fastest.
Arguments:
- next_grad: bfloat16 [512, 1024, 256], P(('lat', 'obs'), None, 'chan'), may hold values from -6 to 6
- pre_act: bfloat16 [512, 1024, 256], P(('lat', 'obs'), None, 'chan'), may hold values from -6 to 6
- legendre: bfloat16 [512, 512, 512], P(('lat', 'obs')), may hold values from -1 to 1, as said below
- order_slots: int32 [512], replicated, may hold values from 0 to 511, as said below
- quad_weights: float32 [512], replicated, may hold values from 0.5 to 1.5
- spectral_gain: float32 [2, 512, 256], P(None, None, 'chan'), may hold values from -5 to 5
- saved_coeffs: bfloat16 [512, 2, 512, 256], P(('lat', 'obs'), None, None, 'chan'), may hold values from -0.029907227 to 0.029907227
- obs_value: bfloat16 [256, 16, 256], P(('lat', 'obs')), may hold values from -16 to 16
- obs_lat_frac: bfloat16 [256, 16, 256], P(('lat', 'obs')), may hold values from 0 to 1
- obs_lon_frac: bfloat16 [256, 16, 256], P(('lat', 'obs')), may hold values from 0 to 1
- obs_corner: int32 [256, 16, 256], P(('lat', 'obs')), may hold values from 0 to 1023
- obs_channel: int32 [256, 16, 256], P(('lat', 'obs')), may hold values from 0 to 255
- slot_counts: int32 [256, 256], P(('lat', 'obs')), may hold values from 0 to 16, as said below
Outputs:
- grid_grad: bfloat16 [512, 1024, 256], P(('lat', 'obs'), None, 'chan')
- gain_grad: float32 [2, 512, 256], P(None, None, 'chan')
The draws below stay inside these ranges and needn't reach their ends.
Inputs may be any that keep to these rules, and one draw needn't show every extreme that they name: `order_slots`: each order from 0 to 511 stands at exactly one slot. `legendre`: entry [s, l, lat] is zero wherever l < order_slots[s]. `slot_counts`: at most 16; in every draw some tile receives 16 live slots from every source shard; slots at or beyond the count carry no observation.
All inputs are finite; a program needn't handle non-finite values.
Results may differ from the reference program's by a relative error of at most 0.0055.
Values may be sent and summed in bfloat16 or wider, within the bound.
No kernel may reach another device: no remote copies, remote signals or barrier semaphores. Data moves between devices by JAX's collectives and lax.ppermute only.
A program may use at most 64 MiB of HBM per device.

```python
import math
import jax
import jax.numpy as jnp
from jax import lax

C = 256
NLON = 1024
L = 512
LAT_DEV = 2
CAP = 16
M = 512
NLAT = 512
SOURCES = 256
DESTS = 256


def shared_orders(key):
    return jax.random.permutation(key, M).astype(jnp.int32)


def draw_order_slots(key, part):
    return shared_orders(key)


def draw_legendre(key, part):
    orders = shared_orders(key)
    key = jax.random.fold_in(key, 3)
    scale = NLAT ** (-0.5)
    values = jnp.clip(jax.random.normal(key, (M, L, NLAT), jnp.float32) * scale, -1.0, 1.0)
    degrees = lax.iota(jnp.int32, L)
    keep = degrees[None, :, None] >= orders[:, None, None]
    return jnp.where(keep, values, 0.0).astype(jnp.bfloat16)


def draw_slot_counts(key, part):
    key = jax.random.fold_in(key, 5)
    base_key, heavy_key, chosen_key = jax.random.split(key, 3)
    base = jax.random.randint(base_key, (SOURCES, DESTS), 0, CAP + 1)
    heavy = jax.random.randint(heavy_key, (DESTS,), 0, 8) == 0
    chosen = jax.random.randint(chosen_key, (), 0, DESTS)
    heavy = heavy | (lax.iota(jnp.int32, DESTS) == chosen)
    return jnp.where(heavy[None, :], CAP, base).astype(jnp.int32)


def touch_ends(result, rng, smallest, largest):
    extent = result.shape
    index_at = [jax.random.randint(jax.random.fold_in(rng, axis), (), 0, extent[axis]) for axis in range(len(extent))]
    result = result.at[tuple(index_at)].set(smallest)
    longest = extent.index(max(extent))
    index_at[longest] = (index_at[longest] + 1) % extent[longest]
    return result.at[tuple(index_at)].set(largest)


def level_of(stream_key, extent, pieces, least, top_value):
    loudness, own = 1.0, jax.random.fold_in(stream_key, 6)
    for position, blocks in pieces:
        heights = jnp.exp(jax.random.uniform(jax.random.fold_in(own, position), (blocks,), jnp.float32, least / len(pieces), top_value / len(pieces)))
        loudness = loudness * jnp.repeat(heights, extent[position] // blocks).reshape([-1 if axis == position else 1 for axis in range(len(extent))])
    return loudness


def normal_values(rng, extent, spread, reach, cuts=(), kind=jnp.bfloat16):
    values = spread * jax.random.normal(rng, extent, jnp.float32)
    if cuts:
        values = values * level_of(rng, extent, cuts, -0.22, 0.18)
    return jnp.clip(values, -reach, reach).astype(kind)


def setup_inputs(seed: int = 0) -> dict:
    key_list = jax.random.split(jax.random.key(seed), 14)
    return {
        "next_grad": normal_values(key_list[0], (NLAT, NLON, C), 1.0, 6.0, ((0, 256), (2, 2))),
        "pre_act": normal_values(key_list[1], (NLAT, NLON, C), 1.0, 6.0, ((0, 256), (2, 2))),
        "legendre": draw_legendre(jax.random.fold_in(key_list[13], 71), 0),
        "order_slots": draw_order_slots(jax.random.fold_in(key_list[13], 71), 0),
        "quad_weights": jnp.clip(jax.random.uniform(key_list[4], (NLAT,), jnp.float32, 0.5, 1.5), 0.5, 1.5),
        "spectral_gain": normal_values(key_list[5], (2, L, C), 1.0, 5.0, ((2, 2),), jnp.float32),
        "saved_coeffs": normal_values(key_list[6], (M, 2, L, C), 0.005, 0.029907227, ((0, 256), (3, 2))),
        "obs_value": normal_values(key_list[7], (SOURCES, CAP, DESTS), 4.0, 16.0, ((0, 256),)),
        "obs_lat_frac": jnp.clip(1.0 * jax.random.uniform(key_list[8], (SOURCES, CAP, DESTS), jnp.float32) ** level_of(key_list[8], (SOURCES, CAP, DESTS), ((0, 256),), -0.2, 0.2), 0.0, 1.0).astype(jnp.bfloat16),
        "obs_lon_frac": jnp.clip(1.0 * jax.random.uniform(key_list[9], (SOURCES, CAP, DESTS), jnp.float32) ** level_of(key_list[9], (SOURCES, CAP, DESTS), ((0, 256),), -0.2, 0.2), 0.0, 1.0).astype(jnp.bfloat16),
        "obs_corner": touch_ends(jax.random.randint(key_list[10], (SOURCES, CAP, DESTS), 0, (LAT_DEV - 1) * NLON), jax.random.fold_in(key_list[10], 1), 0, ((LAT_DEV - 1) * NLON) - 1).astype(jnp.int32),
        "obs_channel": touch_ends(jax.random.randint(key_list[11], (SOURCES, CAP, DESTS), 0, C), jax.random.fold_in(key_list[11], 1), 0, C - 1).astype(jnp.int32),
        "slot_counts": draw_slot_counts(jax.random.fold_in(key_list[13], 71), 0),
    }


def gelu_slope(pre_act):
    values = pre_act.astype(jnp.float32)
    normal_cdf = 0.5 * (1.0 + jax.scipy.special.erf(values * 0.7071067811865476))
    density = jnp.exp(-0.5 * values * values) * 0.3989422804014327
    return normal_cdf + values * density


def zonal_tables(orders, longitudes, lon_count, cos_weight, sin_weight):
    phase = (orders[:, None] * longitudes[None, :]) % lon_count
    angle = phase.astype(jnp.float32) * (2.0 * math.pi / lon_count)
    return (cos_weight * jnp.cos(angle)).astype(jnp.bfloat16), (sin_weight * jnp.sin(angle)).astype(jnp.bfloat16)


def observe(obs_value, obs_lat_frac, obs_lon_frac, obs_corner, obs_channel, slot_counts):
    alive_slots = lax.iota(jnp.int32, CAP)[None, :, None] < slot_counts[:, None, :]
    amounts = jnp.where(alive_slots, obs_value, jnp.zeros((), jnp.bfloat16)).astype(jnp.float32)
    lat_step = obs_lat_frac.astype(jnp.float32)
    lon_step = obs_lon_frac.astype(jnp.float32)
    top = obs_corner // NLON
    left = obs_corner % NLON
    right = (left + 1) % NLON
    tile_rows = lax.iota(jnp.int32, DESTS)[None, None, :] * LAT_DEV + top
    lower = tile_rows * NLON
    upper = lower + NLON
    weights = ((1.0 - lat_step) * (1.0 - lon_step), (1.0 - lat_step) * lon_step, lat_step * (1.0 - lon_step), lat_step * lon_step)
    places = (lower + left, lower + right, upper + left, upper + right)
    field = jnp.zeros((NLAT * NLON * C,), jnp.float32)
    for weight, place in zip(weights, places):
        rounded = lax.optimization_barrier(weight.astype(jnp.bfloat16)).astype(jnp.float32)
        flat_index = (place * C + obs_channel).reshape(-1).astype(jnp.int32)
        field = field.at[flat_index].add((rounded * amounts).reshape(-1))
    return field.reshape(NLAT, NLON, C)


def reference(next_grad, pre_act, legendre, order_slots, quad_weights, spectral_gain, saved_coeffs, obs_value, obs_lat_frac, obs_lon_frac, obs_corner, obs_channel, slot_counts):
    out_grad = next_grad.astype(jnp.float32) + observe(obs_value, obs_lat_frac, obs_lon_frac, obs_corner, obs_channel, slot_counts)
    pre_grad = (out_grad * gelu_slope(pre_act)).astype(jnp.bfloat16)
    orders = lax.iota(jnp.int32, M)
    longitudes = lax.iota(jnp.int32, NLON)
    factor = jnp.where(orders == 0, 1.0, 2.0).astype(jnp.float32)[:, None]
    syn_cos, syn_sin = zonal_tables(orders, longitudes, NLON, factor, -factor)
    pre_wide = pre_grad.astype(jnp.float32)
    real_part = jnp.einsum("mn,knc->mkc", syn_cos.astype(jnp.float32), pre_wide)
    imag_part = jnp.einsum("mn,knc->mkc", syn_sin.astype(jnp.float32), pre_wide)
    fourier_grad = jnp.stack([real_part, imag_part], axis=1).astype(jnp.bfloat16)
    gain_real = spectral_gain[0].astype(jnp.float32)
    gain_imag = spectral_gain[1].astype(jnp.float32)

    def per_slot(summed, slot):
        table = lax.dynamic_index_in_dim(legendre, slot, 0, keepdims=False).astype(jnp.float32)
        order = lax.dynamic_index_in_dim(order_slots, slot, 0, keepdims=False)
        fourier = lax.dynamic_index_in_dim(fourier_grad, order, 0, keepdims=False).astype(jnp.float32)
        up_grad = jnp.einsum("lk,rkc->rlc", table, fourier)
        saved = lax.dynamic_index_in_dim(saved_coeffs, slot, 0, keepdims=False).astype(jnp.float32)
        summed = summed + jnp.stack([up_grad[0] * saved[0] + up_grad[1] * saved[1], up_grad[1] * saved[0] - up_grad[0] * saved[1]])
        coeff_grad = jnp.stack([gain_real * up_grad[0] + gain_imag * up_grad[1], gain_real * up_grad[1] - gain_imag * up_grad[0]])
        coeff_wide = lax.optimization_barrier(coeff_grad.astype(jnp.bfloat16)).astype(jnp.float32)
        lat_grad = (jnp.einsum("lk,rlc->rkc", table, coeff_wide) * quad_weights[None, :, None]).astype(jnp.bfloat16)
        return summed, lat_grad

    gain_grad, lat_grad = lax.scan(per_slot, jnp.zeros((2, L, C), jnp.float32), lax.iota(jnp.int32, M))
    scale = jnp.full((M, 1), 1.0 / NLON, jnp.float32)
    ana_cos, ana_sin = zonal_tables(order_slots, longitudes, NLON, scale, -scale)
    spectral_grad = jnp.einsum("sn,skc->knc", ana_cos.astype(jnp.float32), lat_grad[:, 0].astype(jnp.float32))
    spectral_grad = spectral_grad + jnp.einsum("sn,skc->knc", ana_sin.astype(jnp.float32), lat_grad[:, 1].astype(jnp.float32))
    grid_grad = (out_grad + spectral_grad).astype(jnp.bfloat16)
    return grid_grad, gain_grad
```

```python
import math

import jax
import jax.numpy as jnp
import numpy as np
from jax import lax
from jax.experimental import pallas as pl
from jax.experimental.pallas import tpu as pltpu
from jax.sharding import PartitionSpec as P

BF = jnp.bfloat16
F32 = jnp.float32
NT = (((1,), (1,)), ((), ()))
RANKS = ("lat", "obs")


def dot(left, right):
    return jnp.dot(left, right, preferred_element_type=F32)


def dot_nt(left, right):
    return lax.dot_general(left, right, NT, preferred_element_type=F32)


def call(kernel, out_shape, scratch=(), smem=0, flops=0, limit=40):
    outs = out_shape if isinstance(out_shape, tuple) else (out_shape,)
    moved = sum(math.prod(o.shape) * o.dtype.itemsize for o in outs)

    def run(*args):
        specs = [
            pl.BlockSpec(memory_space=pltpu.SMEM if i < smem else pltpu.VMEM)
            for i in range(len(args))
        ]
        total = moved + sum(math.prod(a.shape) * a.dtype.itemsize for a in args)
        return pl.pallas_call(
            kernel,
            out_shape=out_shape,
            in_specs=specs,
            out_specs=jax.tree.map(lambda _: pl.BlockSpec(memory_space=pltpu.VMEM), out_shape),
            scratch_shapes=list(scratch),
            compiler_params=pltpu.CompilerParams(vmem_limit_bytes=limit << 20),
            cost_estimate=pl.CostEstimate(flops=flops, bytes_accessed=total, transcendentals=0),
        )(*args)

    return run


def iota(shape, axis):
    return lax.broadcasted_iota(jnp.int32, shape, axis)


def pack_kernel(base_ref, value_ref, lat_ref, lon_ref, corner_ref, chan_ref, count_ref, out_ref):
    capacity, tiles = value_ref.shape
    alive = iota((capacity, tiles), 0) < count_ref[...]
    value = jnp.where(alive, value_ref[...].astype(F32), 0.0)
    corner = corner_ref[...]
    fields = [
        value,
        lat_ref[...].astype(F32),
        lon_ref[...].astype(F32),
        (corner // 32).astype(F32),
        (corner % 32).astype(F32),
        (chan_ref[...] - base_ref[0]).astype(F32),
        jnp.zeros((128 - 6 * capacity, tiles), F32),
    ]
    out_ref[...] = jnp.concatenate(fields, axis=0).T.astype(BF)


def ready_kernel(pre_ref, legendre_ref, quad_ref, slope_ref, up_ref, down_ref, weight_ref):
    values = pre_ref[...].astype(F32)
    cdf = 0.5 * (1.0 + lax.erf(values * 0.7071067811865476))
    density = jnp.exp(-0.5 * values * values) * 0.3989422804014327
    slope_ref[...] = cdf + values * density
    lats = legendre_ref.shape[2]
    half = lats // 2
    place = iota((lats, lats), 0)
    lat = iota((lats, lats), 1)
    pick = ((place % half) * 2 + place // half == lat).astype(BF)
    for s in range(legendre_ref.shape[0]):
        table = legendre_ref[s]
        up_ref[s] = dot_nt(table, pick).astype(BF)
        down_ref[s] = dot_nt(pick, table).astype(BF)
    for k in range(2):
        column = quad_ref[:, k : k + 1]
        weight_ref[k * half : (k + 1) * half, :] = jnp.broadcast_to(column, (half, 128))


def synth_kernel(
    slots_ref, next_ref, slope_ref, table_ref, order_ref, sent_ref, grad_ref, rows_ref, cols_ref, acc_ref, msg_ref
):
    lat_dev, lons, width = next_ref.shape
    ranks = slots_ref.shape[0]
    capacity = 16
    fields = slots_ref[...].astype(F32).T
    value = fields[0:16]
    lat_step = fields[16:32]
    lon_step = fields[32:48]
    corner = (fields[48:64] * 32.0 + fields[64:80]).astype(jnp.int32)
    chan = fields[80:96].astype(jnp.int32)
    weights = (
        (1.0 - lat_step) * (1.0 - lon_step),
        lat_step * (1.0 - lon_step),
        (1.0 - lat_step) * lon_step,
        lat_step * lon_step,
    )
    chan_ids = iota((width, ranks), 0)
    for p in range(capacity):
        hit = chan_ids == chan[p : p + 1]
        for k in range(4):
            cols_ref[k * width : (k + 1) * width, p * ranks : (p + 1) * ranks] = jnp.where(
                hit, weights[k][p : p + 1], 0.0
            ).astype(BF)
    block = 256
    for j in range(lons // block):
        lon_ids = iota((block, ranks), 0) + j * block
        for p in range(capacity):
            rows_ref[:, p * ranks : (p + 1) * ranks] = jnp.where(
                lon_ids == corner[p : p + 1], value[p : p + 1], 0.0
            ).astype(BF)
        found = dot_nt(rows_ref[...], cols_ref[...])
        acc_ref[8 + j * block : 8 + (j + 1) * block, :] = found
    acc_ref[7:8, 2 * width :] = acc_ref[7 + lons : 8 + lons, 2 * width :]
    halves = []
    for h in range(2):
        at = h * (lons // 2)
        parts = []
        for k in range(lat_dev):
            here = acc_ref[8 + at : 8 + at + lons // 2, k * width : (k + 1) * width]
            left = acc_ref[7 + at : 7 + at + lons // 2, (2 + k) * width : (3 + k) * width]
            total = next_ref[k, at : at + lons // 2, :].astype(F32) + (here + left)
            grad_ref[k, at : at + lons // 2, :] = total
            parts.append((total * slope_ref[k, at : at + lons // 2, :]).astype(BF))
        halves.extend(parts)
    field = jnp.concatenate(halves, axis=1)
    orders = table_ref.shape[1]
    order_ids = iota((orders, 1), 0)
    sign = jnp.where(order_ids % 2 == 0, 1.0, -1.0)
    scale = jnp.where(order_ids == 0, 1.0, 2.0)
    pair = lat_dev * width
    for r in range(2):
        both = dot(table_ref[r], field)
        total = (both[:, :pair] + sign * both[:, pair:]) * (scale if r == 0 else -scale)
        total = total.astype(BF)
        for s in range(2):
            chosen = (iota((ranks, orders), 1) == order_ref[:, s : s + 1]).astype(BF)
            placed = dot(chosen, total)
            for k in range(lat_dev):
                row = s * 4 + r * 2 + k
                msg_ref[pl.ds(row, ranks, stride=8), :] = placed[:, k * width : (k + 1) * width]
    sent_ref[...] = msg_ref[...].reshape(ranks, 8, width).astype(BF)


def legendre_kernel(
    got_ref, up_ref, down_ref, weight_ref, saved_ref, gain_ref, first_ref, second_ref, msg_ref
):
    ranks, rows, width = got_ref.shape
    msg_ref[...] = got_ref[...].astype(F32).reshape(ranks * rows, width)
    gain_real = gain_ref[0]
    gain_imag = gain_ref[1]
    terms = [None, None]
    columns = []
    for s in range(2):
        parts = []
        for r in range(2):
            lanes = [
                msg_ref[pl.ds(s * 4 + r * 2 + k, ranks, stride=8), :].astype(BF) for k in range(2)
            ]
            parts.append(jnp.concatenate(lanes, axis=0))
        columns.append(jnp.concatenate(parts, axis=1))
    for s in range(2):
        found = dot(up_ref[s], columns[s])
        real = found[:, :width]
        imag = found[:, width:]
        saved_real = saved_ref[s, 0].astype(F32)
        saved_imag = saved_ref[s, 1].astype(F32)
        new = (real * saved_real + imag * saved_imag, imag * saved_real - real * saved_imag)
        terms = [n if t is None else t + n for t, n in zip(terms, new)]
        coeff = jnp.concatenate(
            [gain_real * real + gain_imag * imag, gain_real * imag - gain_imag * real], axis=1
        ).astype(BF)
        lat_grad = dot(down_ref[s], coeff)
        for r in range(2):
            weighted = lat_grad[:, r * width : (r + 1) * width] * weight_ref[...]
            for k in range(2):
                msg_ref[pl.ds(r * 2 + k, ranks, stride=8), :] = weighted[k * ranks : (k + 1) * ranks]
        if s == 1:
            second_ref[...] = msg_ref[...].reshape(ranks, 8, width).astype(BF)
        else:
            first_ref[...] = msg_ref[...].reshape(ranks, 8, width).astype(BF)
    for g in range(2):
        for h in range(2):
            msg_ref[pl.ds(4 + g * 2 + h, ranks, stride=8), :] = terms[g][h * ranks : (h + 1) * ranks]
    whole = msg_ref[...].reshape(ranks, 8, width).astype(BF)
    row = iota((ranks, 8, width), 1)
    first_ref[...] = jnp.where(row < 4, first_ref[...].astype(F32), whole.astype(F32)).astype(BF)


def share_kernel(got_ref, half_ref, sent_ref):
    total = jnp.sum(got_ref[...].astype(F32), axis=0, keepdims=True)
    row = iota(got_ref.shape, 1)
    sent_ref[...] = jnp.where(row < 4, half_ref[...].astype(F32), total).astype(BF)


def spectral_part(got_ref, order_ref, table_ref, msg_ref, s):
    ranks, rows, width = got_ref.shape
    orders = table_ref.shape[1]
    msg_ref[...] = got_ref[...].astype(F32).reshape(ranks * rows, width)
    order_ids = iota((orders, 1), 0)
    sign = jnp.where(order_ids % 2 == 0, 1.0, -1.0)
    chosen = (iota((orders, ranks), 0) == order_ref[s : s + 1, :]).astype(BF)
    total = None
    for r in range(2):
        lanes = [msg_ref[pl.ds(r * 2 + k, ranks, stride=8), :].astype(BF) for k in range(2)]
        placed = dot(chosen, jnp.concatenate(lanes, axis=1))
        both = jnp.concatenate([placed, placed * sign], axis=1).astype(BF)
        part = dot(table_ref[r], both)
        total = part if total is None else total - part
    return total * (1.0 / (2 * orders))


def first_kernel(got_ref, order_ref, table_ref, grad_ref, out_ref, msg_ref):
    lat_dev, lons, width = grad_ref.shape
    part = spectral_part(got_ref, order_ref, table_ref, msg_ref, 0)
    half = lons // 2
    for h in range(2):
        for k in range(lat_dev):
            at = (h * lat_dev + k) * width
            out_ref[k, h * half : (h + 1) * half, :] = (
                grad_ref[k, h * half : (h + 1) * half, :] + part[:, at : at + width]
            )


def second_kernel(got_ref, order_ref, table_ref, grad_ref, out_ref, gain_ref, msg_ref):
    lat_dev, lons, width = grad_ref.shape
    ranks = got_ref.shape[0]
    part = spectral_part(got_ref, order_ref, table_ref, msg_ref, 1)
    half = lons // 2
    for h in range(2):
        for k in range(lat_dev):
            at = (h * lat_dev + k) * width
            out_ref[k, h * half : (h + 1) * half, :] = (
                grad_ref[k, h * half : (h + 1) * half, :] + part[:, at : at + width]
            ).astype(BF)
    for g in range(2):
        for h in range(2):
            gain_ref[g, h * ranks : (h + 1) * ranks, :] = msg_ref[
                pl.ds(4 + g * 2 + h, ranks, stride=8), :
            ]


def exchange(message):
    return lax.all_to_all(message, RANKS, split_axis=0, concat_axis=0, tiled=True)


def on_device(
    next_grad,
    pre_act,
    legendre,
    order_slots,
    quad_weights,
    spectral_gain,
    saved_coeffs,
    obs_value,
    obs_lat_frac,
    obs_lon_frac,
    obs_corner,
    obs_channel,
    slot_counts,
):
    lat_dev, lons, width = next_grad.shape
    slot_dev, degrees, lats = legendre.shape
    orders = order_slots.shape[0]
    ranks = lax.axis_size("lat") * lax.axis_size("obs")
    shape = jax.ShapeDtypeStruct

    index = np.arange(orders)
    angle = ((index[:, None] * index[None, :]) % lons).astype(np.float32) * np.float32(
        2.0 * math.pi / lons
    )
    table = jnp.asarray(np.stack([np.cos(angle), np.sin(angle)]).astype(jnp.bfloat16))

    base = (lax.axis_index("chan") * width).astype(jnp.int32).reshape(1)
    packed = call(pack_kernel, shape((ranks, 128), BF), smem=1)(
        base,
        obs_value[0],
        obs_lat_frac[0],
        obs_lon_frac[0],
        obs_corner[0],
        obs_channel[0],
        slot_counts,
    )
    slots = exchange(packed.reshape(ranks, 1, 128)).reshape(ranks, 128)

    slope, up_table, down_table, weight = call(
        ready_kernel,
        (
            shape(next_grad.shape, F32),
            shape(legendre.shape, BF),
            shape((slot_dev, lats, degrees), BF),
            shape((lats, 128), F32),
        ),
        flops=4 * 2 * 512**3,
    )(pre_act, legendre, quad_weights.reshape(ranks, 2))

    order_columns = order_slots.reshape(ranks, 2)
    order_rows = order_columns.T
    message = shape((ranks, 8, width), BF)
    rows = pltpu.VMEM((ranks * 8, width), F32)
    sent, out_grad = call(
        synth_kernel,
        (message, shape(next_grad.shape, F32)),
        scratch=[
            pltpu.VMEM((256, 16 * ranks), BF),
            pltpu.VMEM((4 * width, 16 * ranks), BF),
            pltpu.VMEM((lons + 8, 4 * width), F32),
            rows,
        ],
        flops=2 * 1024 * 4096 * 512,
    )(slots, next_grad, slope, table, order_columns)
    by_order = exchange(sent)
    first, second = call(legendre_kernel, (message, message), scratch=[rows], flops=2 * 512**3 * 4)(
        by_order, up_table, down_table, weight, saved_coeffs, spectral_gain
    )
    first = exchange(first)
    second = exchange(call(share_kernel, message)(first, second))
    partial = call(first_kernel, shape(next_grad.shape, F32), scratch=[rows], flops=2 * 512**3 * 3)(
        first, order_rows, table, out_grad
    )
    return call(
        second_kernel,
        (shape(next_grad.shape, BF), shape((2, degrees, width), F32)),
        scratch=[rows],
        flops=2 * 512**3 * 3,
    )(second, order_rows, table, partial)


def solution(mesh):
    ranks = P(RANKS, None, None)
    in_specs = (
        P(RANKS, None, "chan"),
        P(RANKS, None, "chan"),
        ranks,
        P(),
        P(),
        P(None, None, "chan"),
        P(RANKS, None, None, "chan"),
        ranks,
        ranks,
        ranks,
        ranks,
        ranks,
        P(RANKS, None),
    )
    out_specs = (P(RANKS, None, "chan"), P(None, None, "chan"))
    return jax.shard_map(
        on_device, mesh=mesh, in_specs=in_specs, out_specs=out_specs, check_vma=False
    )
```

```python
import math

import jax
import jax.numpy as jnp
import numpy as np
from jax import lax
from jax.experimental import pallas as pl
from jax.experimental.pallas import tpu as pltpu
from jax.sharding import PartitionSpec as P

BF = jnp.bfloat16
F32 = jnp.float32
NT = (((1,), (1,)), ((), ()))
RANKS = ("lat", "obs")


def dot(left, right):
    return jnp.dot(left, right, preferred_element_type=F32)


def dot_nt(left, right):
    return lax.dot_general(left, right, NT, preferred_element_type=F32)


def call(kernel, out_shape, scratch=(), smem=0, far=False, far_out=False, flops=0, limit=16):
    outs = out_shape if isinstance(out_shape, tuple) else (out_shape,)
    moved = sum(math.prod(o.shape) * o.dtype.itemsize for o in outs)

    def run(*args):
        rest = pltpu.HBM if far else pltpu.VMEM
        specs = [
            pl.BlockSpec(memory_space=pltpu.SMEM if i < smem else rest) for i in range(len(args))
        ]
        total = moved + sum(math.prod(a.shape) * a.dtype.itemsize for a in args)
        return pl.pallas_call(
            kernel,
            out_shape=out_shape,
            in_specs=specs,
            out_specs=jax.tree.map(
                lambda _: pl.BlockSpec(memory_space=pltpu.HBM if far_out else pltpu.VMEM), out_shape
            ),
            scratch_shapes=list(scratch),
            compiler_params=pltpu.CompilerParams(vmem_limit_bytes=limit << 20),
            cost_estimate=pl.CostEstimate(flops=flops, bytes_accessed=total, transcendentals=0),
        )(*args)

    return run


def iota(shape, axis):
    return lax.broadcasted_iota(jnp.int32, shape, axis)


def pack_kernel(base_ref, *refs):
    sources, out_ref, buffers, sems = refs[:6], refs[6], refs[7:13], refs[13]
    copies = [
        pltpu.make_async_copy(source, buffer, sems.at[i])
        for i, (source, buffer) in enumerate(zip(sources, buffers))
    ]
    for copy in copies:
        copy.start()
    for copy in copies:
        copy.wait()
    value, lat_frac, lon_frac, corner, chan, counts = [buffer[...] for buffer in buffers]
    capacity, tiles = value.shape
    alive = iota((capacity, tiles), 0) < counts
    fields = [
        jnp.where(alive, value.astype(F32), 0.0),
        lat_frac.astype(F32),
        lon_frac.astype(F32),
        corner.astype(F32),
        (chan - base_ref[0]).astype(F32),
        jnp.zeros((128 - 5 * capacity, tiles), F32),
    ]
    out_ref[...] = jnp.concatenate(fields, axis=0).T


def ready_kernel(
    pre_ref, legendre_ref, quad_ref, order_ref, slope_ref, up_ref, down_ref, weight_ref, cols_ref, rows_ref
):
    values = pre_ref[...].astype(F32)
    cdf = 0.5 * (1.0 + lax.erf(values * 0.7071067811865476))
    density = jnp.exp(-0.5 * values * values) * 0.3989422804014327
    slope_ref[...] = cdf + values * density
    lats = legendre_ref.shape[2]
    half = lats // 2
    place = iota((lats, lats), 0)
    chosen = (place % half) * 2 + place // half == iota((lats, lats), 1)
    pick = chosen.astype(BF)
    for s in range(legendre_ref.shape[0]):
        table = legendre_ref[s]
        up_ref[s] = dot_nt(table, pick).astype(BF)
        down_ref[s] = dot_nt(pick, table).astype(BF)
    quad = jnp.sum(jnp.where(chosen, quad_ref[...], 0.0), axis=1, keepdims=True)
    weight_ref[...] = jnp.broadcast_to(quad, weight_ref.shape)
    order = jnp.where(chosen, order_ref[...].astype(F32), 0.0)
    order = jnp.sum(order, axis=1, keepdims=True).astype(jnp.int32)
    order = jnp.broadcast_to(order, cols_ref.shape)
    cols_ref[...] = order
    rows_ref[...] = order.T[:8]


def tall(row, count):
    block = jnp.broadcast_to(row, (16, row.shape[1])).astype(BF)
    return jnp.concatenate([block] * (count // 16), axis=0)


def synth_kernel(
    slots_ref, next_ref, slope_ref, table_ref, order_ref, sent_ref, grad_ref, rows_ref, cols_ref, field_ref, msg_ref
):
    lat_dev, lons, width = next_ref.shape
    ranks = slots_ref.shape[0]
    capacity = 16
    groups = lons // 4
    fields = slots_ref[...].T
    value = fields[0:16]
    lat_step = fields[16:32]
    lon_step = fields[32:48]
    corner = fields[48:64].astype(jnp.int32)
    chan = fields[64:80]
    group = (corner // 4).astype(F32)
    place = corner % 4
    at_left = ((1.0 - lat_step) * (1.0 - lon_step), lat_step * (1.0 - lon_step))
    at_right = ((1.0 - lat_step) * lon_step, lat_step * lon_step)
    weights = [
        jnp.where(place == j, at_left[k], 0.0) + jnp.where(place == j - 1, at_right[k], 0.0)
        for j in range(5)
        for k in range(lat_dev)
    ]
    chan_ids = iota((width, ranks), 0).astype(F32).astype(BF)
    group_ids = iota((groups, ranks), 0).astype(F32).astype(BF)
    nothing = jnp.zeros((), BF)
    for p in range(capacity):
        span = slice(p * ranks, (p + 1) * ranks)
        rows_ref[:, span] = jnp.where(
            group_ids == tall(group[p : p + 1], groups), tall(value[p : p + 1], groups), nothing
        )
        hit = chan_ids == tall(chan[p : p + 1], width)
        for i, weight in enumerate(weights):
            cols_ref[i * width : (i + 1) * width, span] = jnp.where(
                hit, tall(weight[p : p + 1], width), nothing
            )
    pair = lat_dev * width
    found = [
        dot_nt(rows_ref[...], cols_ref[j * pair : (j + 1) * pair, :]) for j in range(5)
    ]
    found[0] = found[0] + pltpu.roll(found[4], 1, 0)
    for j in range(4):
        for k in range(lat_dev):
            field_ref[k, pl.ds(j, groups, stride=4), :] = found[j][:, k * width : (k + 1) * width]
    halves = []
    for h in range(2):
        at = h * (lons // 2)
        parts = []
        for k in range(lat_dev):
            total = next_ref[k, at : at + lons // 2, :].astype(F32) + field_ref[
                k, at : at + lons // 2, :
            ]
            grad_ref[k, at : at + lons // 2, :] = total
            parts.append((total * slope_ref[k, at : at + lons // 2, :]).astype(BF))
        halves.extend(parts)
    field = jnp.concatenate(halves, axis=1)
    orders = table_ref.shape[1]
    order_ids = iota((orders, 1), 0)
    sign = jnp.where(order_ids % 2 == 0, 1.0, -1.0)
    scale = jnp.where(order_ids == 0, 1.0, 2.0)
    for r in range(2):
        both = dot(table_ref[r], field)
        total = (both[:, :pair] + sign * both[:, pair:]) * (scale if r == 0 else -scale)
        total = total.astype(BF)
        for s in range(2):
            chosen = (iota((ranks, orders), 1) == order_ref[s * ranks : (s + 1) * ranks, 0:1]).astype(BF)
            placed = dot(chosen, total)
            for k in range(lat_dev):
                row = s * 4 + r * 2 + k
                msg_ref[pl.ds(row, ranks, stride=8), :] = placed[:, k * width : (k + 1) * width]
    sent_ref[...] = msg_ref[...].reshape(ranks, 8, width).astype(BF)


def legendre_kernel(
    got_ref, up_ref, down_ref, weight_ref, saved_ref, gain_ref, first_ref, second_ref, msg_ref, out_ref
):
    ranks, rows, width = got_ref.shape
    msg_ref[...] = got_ref[...].astype(F32).reshape(ranks * rows, width)
    gain_real = gain_ref[0]
    gain_imag = gain_ref[1]
    terms = [None, None]
    for s in range(2):
        parts = []
        for r in range(2):
            lanes = [
                msg_ref[pl.ds(s * 4 + r * 2 + k, ranks, stride=8), :].astype(BF) for k in range(2)
            ]
            parts.append(jnp.concatenate(lanes, axis=0))
        found = dot(up_ref[s], jnp.concatenate(parts, axis=1))
        real = found[:, :width]
        imag = found[:, width:]
        saved_real = saved_ref[s, 0].astype(F32)
        saved_imag = saved_ref[s, 1].astype(F32)
        new = (real * saved_real + imag * saved_imag, imag * saved_real - real * saved_imag)
        terms = [n if t is None else t + n for t, n in zip(terms, new)]
        coeff = jnp.concatenate(
            [gain_real * real + gain_imag * imag, gain_real * imag - gain_imag * real], axis=1
        ).astype(BF)
        lat_grad = dot(down_ref[s], coeff)
        for r in range(2):
            weighted = lat_grad[:, r * width : (r + 1) * width] * weight_ref[...]
            for k in range(2):
                out_ref[s, pl.ds(r * 2 + k, ranks, stride=8), :] = weighted[
                    k * ranks : (k + 1) * ranks
                ]
    for g in range(2):
        for h in range(2):
            part = terms[g][h * ranks : (h + 1) * ranks]
            for s in range(2):
                out_ref[s, pl.ds(4 + g * 2 + h, ranks, stride=8), :] = part
    first_ref[...] = out_ref[0].reshape(ranks, rows, width).astype(BF)
    second_ref[...] = out_ref[1].reshape(ranks, rows, width).astype(BF)


def share_kernel(got_ref, half_ref, sent_ref):
    ranks, rows, width = got_ref.shape
    part = ranks // 16
    total = got_ref[0:part].astype(F32)
    for i in range(1, 16):
        total = total + got_ref[i * part : (i + 1) * part].astype(F32)
    total = jnp.sum(total, axis=0, keepdims=True).astype(BF)
    sent_ref[...] = jnp.where(iota(got_ref.shape, 1) < 4, half_ref[...], total)


def natural(msg_ref, order_ref, orders, s):
    ranks = msg_ref.shape[0] // 8
    sign = jnp.where(iota((orders, 1), 0) % 2 == 0, 1.0, -1.0)
    chosen = (iota((orders, ranks), 0) == order_ref[0:1, s * ranks : (s + 1) * ranks]).astype(BF)
    both = []
    for r in range(2):
        lanes = [msg_ref[pl.ds(r * 2 + k, ranks, stride=8), :].astype(BF) for k in range(2)]
        placed = dot(chosen, jnp.concatenate(lanes, axis=1))
        both.append(jnp.concatenate([placed, placed * sign], axis=1).astype(BF))
    return both


def first_kernel(got_ref, order_ref, table_ref, grad_ref, out_ref, msg_ref):
    lat_dev, lons, width = grad_ref.shape
    half = lons // 2
    msg_ref[...] = got_ref[...].astype(F32).reshape(msg_ref.shape)
    both = natural(msg_ref, order_ref, half, 0)
    part = (dot(table_ref[0], both[0]) - dot(table_ref[1], both[1])) * (1.0 / lons)
    for h in range(2):
        span = slice(h * half, (h + 1) * half)
        for k in range(lat_dev):
            at = (h * lat_dev + k) * width
            out_ref[k, span, :] = grad_ref[k, span, :] + part[:, at : at + width]


def second_kernel(got_ref, order_ref, table_ref, grad_ref, out_ref, gain_ref, msg_ref, field_ref, share_ref, sems):
    lat_dev, lons, width = grad_ref.shape
    ranks = got_ref.shape[0]
    half = lons // 2
    msg_ref[...] = got_ref[...].astype(F32).reshape(msg_ref.shape)
    for g in range(2):
        for h in range(2):
            share_ref[g, h * ranks : (h + 1) * ranks, :] = msg_ref[
                pl.ds(4 + g * 2 + h, ranks, stride=8), :
            ]
    copies = [pltpu.make_async_copy(share_ref, gain_ref, sems.at[0])]
    copies[0].start()
    both = natural(msg_ref, order_ref, half, 1)
    block = half // 4
    for i in range(4):
        rows = slice(i * block, (i + 1) * block)
        part = dot(table_ref[0, rows, :], both[0]) - dot(table_ref[1, rows, :], both[1])
        part = part * (1.0 / lons)
        for h in range(2):
            span = slice(h * half + i * block, h * half + (i + 1) * block)
            for k in range(lat_dev):
                at = (h * lat_dev + k) * width
                field_ref[k, span, :] = (grad_ref[k, span, :] + part[:, at : at + width]).astype(BF)
            copies.append(
                pltpu.make_async_copy(
                    field_ref.at[:, span, :], out_ref.at[:, span, :], sems.at[len(copies)]
                )
            )
            copies[-1].start()
    for copy in copies:
        copy.wait()


def exchange(message):
    return lax.all_to_all(message, RANKS, split_axis=0, concat_axis=0, tiled=True)


def on_device(
    next_grad,
    pre_act,
    legendre,
    order_slots,
    quad_weights,
    spectral_gain,
    saved_coeffs,
    obs_value,
    obs_lat_frac,
    obs_lon_frac,
    obs_corner,
    obs_channel,
    slot_counts,
):
    lat_dev, lons, width = next_grad.shape
    slot_dev, degrees, lats = legendre.shape
    orders = order_slots.shape[0]
    ranks = lax.axis_size("lat") * lax.axis_size("obs")
    shape = jax.ShapeDtypeStruct

    index = np.arange(orders)
    angle = ((index[:, None] * index[None, :]) % lons).astype(np.float32) * np.float32(
        2.0 * math.pi / lons
    )
    table = jnp.asarray(np.stack([np.cos(angle), np.sin(angle)]).astype(jnp.bfloat16))

    base = (lax.axis_index("chan") * width).astype(jnp.int32).reshape(1)
    slot_args = (
        obs_value[0],
        obs_lat_frac[0],
        obs_lon_frac[0],
        obs_corner[0],
        obs_channel[0],
        slot_counts,
    )
    slots = exchange(
        call(
            pack_kernel,
            shape((ranks, 128), F32),
            scratch=[pltpu.VMEM(a.shape, a.dtype) for a in slot_args]
            + [pltpu.SemaphoreType.DMA((len(slot_args),))],
            smem=1,
            far=True,
            limit=60,
        )(base, *slot_args)
    )

    slope, up_table, down_table, weight, order_columns, order_rows = call(
        ready_kernel,
        (
            shape(next_grad.shape, F32),
            shape(legendre.shape, BF),
            shape((slot_dev, lats, degrees), BF),
            shape((lats, 128), F32),
            shape((orders, 128), jnp.int32),
            shape((8, orders), jnp.int32),
        ),
        flops=4 * 2 * 512**3,
    )(pre_act, legendre, quad_weights.reshape(1, lats), order_slots.reshape(1, orders))

    message = shape((ranks, 8, width), BF)
    rows = pltpu.VMEM((ranks * 8, width), F32)
    sent, out_grad = call(
        synth_kernel,
        (message, shape(next_grad.shape, F32)),
        scratch=[
            pltpu.VMEM((lons // 4, 16 * ranks), BF),
            pltpu.VMEM((10 * width, 16 * ranks), BF),
            pltpu.VMEM((lat_dev, lons, width), F32),
            rows,
        ],
        flops=2 * 1024 * 4096 * 512,
        limit=32,
    )(slots, next_grad, slope, table, order_columns)
    by_order = exchange(sent)
    first, second = call(legendre_kernel, (message, message), scratch=[rows, pltpu.VMEM((2, ranks * 8, width), F32)], flops=2 * 512**3 * 4)(
        by_order, up_table, down_table, weight, saved_coeffs, spectral_gain
    )
    first = exchange(first)
    second = exchange(call(share_kernel, message)(first, second))
    partial = call(first_kernel, shape(next_grad.shape, F32), scratch=[rows], flops=2 * 512**3 * 3)(
        first, order_rows, table, out_grad
    )
    outs = (shape(next_grad.shape, BF), shape((2, degrees, width), F32))
    return call(
        second_kernel,
        outs,
        scratch=[rows]
        + [pltpu.VMEM(o.shape, o.dtype) for o in outs]
        + [pltpu.SemaphoreType.DMA((9,))],
        far_out=True,
        flops=2 * 512**3 * 3,
    )(second, order_rows, table, partial)


def solution(mesh):
    ranks = P(RANKS, None, None)
    in_specs = (
        P(RANKS, None, "chan"),
        P(RANKS, None, "chan"),
        ranks,
        P(),
        P(),
        P(None, None, "chan"),
        P(RANKS, None, None, "chan"),
        ranks,
        ranks,
        ranks,
        ranks,
        ranks,
        P(RANKS, None),
    )
    out_specs = (P(RANKS, None, "chan"), P(None, None, "chan"))
    return jax.shard_map(
        on_device, mesh=mesh, in_specs=in_specs, out_specs=out_specs, check_vma=False
    )
```

```python
import math

import jax
import jax.numpy as jnp
import numpy as np
from jax import lax
from jax.experimental import pallas as pl
from jax.experimental.pallas import tpu as pltpu
from jax.sharding import PartitionSpec as P

BF = jnp.bfloat16
F32 = jnp.float32
NT = (((1,), (1,)), ((), ()))
RANKS = ("lat", "obs")


def dot(left, right):
    return jnp.dot(left, right, preferred_element_type=F32)


def dot_nt(left, right):
    return lax.dot_general(left, right, NT, preferred_element_type=F32)


def call(kernel, out_shape, scratch=(), smem=0, far=(), far_out=False, flops=0, limit=16):
    outs = out_shape if isinstance(out_shape, tuple) else (out_shape,)
    moved = sum(math.prod(o.shape) * o.dtype.itemsize for o in outs)

    def run(*args):
        specs = [
            pl.BlockSpec(
                memory_space=pltpu.SMEM if i < smem else pltpu.HBM if i in far else pltpu.VMEM
            )
            for i in range(len(args))
        ]
        total = moved + sum(math.prod(a.shape) * a.dtype.itemsize for a in args)
        return pl.pallas_call(
            kernel,
            out_shape=out_shape,
            in_specs=specs,
            out_specs=jax.tree.map(
                lambda _: pl.BlockSpec(memory_space=pltpu.HBM if far_out else pltpu.VMEM), out_shape
            ),
            scratch_shapes=list(scratch),
            compiler_params=pltpu.CompilerParams(vmem_limit_bytes=limit << 20),
            cost_estimate=pl.CostEstimate(flops=flops, bytes_accessed=total, transcendentals=0),
        )(*args)

    return run


def buffers_for(arrays):
    return [pltpu.VMEM(a.shape, a.dtype) for a in arrays] + [pltpu.SemaphoreType.DMA((len(arrays),))]


def start_copies(sources, targets, sems):
    copies = [
        pltpu.make_async_copy(source, target, sems.at[i])
        for i, (source, target) in enumerate(zip(sources, targets))
    ]
    for copy in copies:
        copy.start()
    return copies


def iota(shape, axis):
    return lax.broadcasted_iota(jnp.int32, shape, axis)


def pack_kernel(base_ref, *refs):
    sources, out_ref, buffers, sems = refs[:6], refs[6], refs[7:13], refs[13]
    for copy in start_copies(sources, buffers, sems):
        copy.wait()
    value, lat_frac, lon_frac, corner, chan, counts = [buffer[...] for buffer in buffers]
    capacity, tiles = value.shape
    alive = iota((capacity, tiles), 0) < counts
    fields = [
        jnp.where(alive, value.astype(F32), 0.0),
        lat_frac.astype(F32),
        lon_frac.astype(F32),
        corner.astype(F32),
        (chan - base_ref[0]).astype(F32),
        jnp.zeros((128 - 5 * capacity, tiles), F32),
    ]
    out_ref[...] = jnp.concatenate(fields, axis=0).T


def ready_kernel(*refs):
    sources, results = refs[:2], refs[2:5]
    legendre_ref, quad_ref, in_sems, up_ref, down_ref, weight_ref, out_sems = refs[5:]
    for copy in start_copies(sources, (legendre_ref, quad_ref), in_sems):
        copy.wait()
    lats = legendre_ref.shape[2]
    half = lats // 2
    place = iota((lats, lats), 0)
    chosen = (place % half) * 2 + place // half == iota((lats, lats), 1)
    quad = jnp.sum(jnp.where(chosen, quad_ref[...], 0.0), axis=1, keepdims=True)
    weight_ref[...] = jnp.broadcast_to(quad, weight_ref.shape)
    pick = chosen.astype(BF)
    for s in range(legendre_ref.shape[0]):
        up_ref[s] = dot_nt(legendre_ref[s], pick).astype(BF)
        down_ref[s] = dot_nt(pick, legendre_ref[s]).astype(BF)
    for copy in start_copies((up_ref, down_ref, weight_ref), results, out_sems):
        copy.wait()


def tall(row, count):
    block = jnp.broadcast_to(row, (16, row.shape[1])).astype(BF)
    return jnp.concatenate([block] * (count // 16), axis=0)


def synth_kernel(
    slots_ref, next_ref, pre_ref, table_ref, order_ref, sent_ref, grad_ref, slope_ref, rows_ref, cols_ref, field_ref, msg_ref
):
    values = pre_ref[...].astype(F32)
    cdf = 0.5 * (1.0 + lax.erf(values * 0.7071067811865476))
    density = jnp.exp(-0.5 * values * values) * 0.3989422804014327
    slope_ref[...] = cdf + values * density
    lat_dev, lons, width = next_ref.shape
    ranks = slots_ref.shape[0]
    capacity = 16
    groups = lons // 4
    fields = slots_ref[...].T
    value = fields[0:16]
    lat_step = fields[16:32]
    lon_step = fields[32:48]
    corner = fields[48:64].astype(jnp.int32)
    chan = fields[64:80]
    group = (corner // 4).astype(F32)
    place = corner % 4
    at_left = ((1.0 - lat_step) * (1.0 - lon_step), lat_step * (1.0 - lon_step))
    at_right = ((1.0 - lat_step) * lon_step, lat_step * lon_step)
    weights = [
        jnp.where(place == j, at_left[k], 0.0) + jnp.where(place == j - 1, at_right[k], 0.0)
        for j in range(5)
        for k in range(lat_dev)
    ]
    chan_ids = iota((width, ranks), 0).astype(F32).astype(BF)
    group_ids = iota((groups, ranks), 0).astype(F32).astype(BF)
    nothing = jnp.zeros((), BF)
    for p in range(capacity):
        span = slice(p * ranks, (p + 1) * ranks)
        rows_ref[:, span] = jnp.where(
            group_ids == tall(group[p : p + 1], groups), tall(value[p : p + 1], groups), nothing
        )
        hit = chan_ids == tall(chan[p : p + 1], width)
        for i, weight in enumerate(weights):
            cols_ref[i * width : (i + 1) * width, span] = jnp.where(
                hit, tall(weight[p : p + 1], width), nothing
            )
    pair = lat_dev * width
    found = [
        dot_nt(rows_ref[...], cols_ref[j * pair : (j + 1) * pair, :]) for j in range(5)
    ]
    found[0] = found[0] + pltpu.roll(found[4], 1, 0)
    for j in range(4):
        for k in range(lat_dev):
            field_ref[k, pl.ds(j, groups, stride=4), :] = found[j][:, k * width : (k + 1) * width]
    halves = []
    for h in range(2):
        at = h * (lons // 2)
        parts = []
        for k in range(lat_dev):
            total = next_ref[k, at : at + lons // 2, :].astype(F32) + field_ref[
                k, at : at + lons // 2, :
            ]
            grad_ref[k, at : at + lons // 2, :] = total
            parts.append((total * slope_ref[k, at : at + lons // 2, :]).astype(BF))
        halves.extend(parts)
    field = jnp.concatenate(halves, axis=1)
    orders = table_ref.shape[1]
    order_ids = iota((orders, 1), 0)
    sign = jnp.where(order_ids % 2 == 0, 1.0, -1.0)
    scale = jnp.where(order_ids == 0, 1.0, 2.0)
    for r in range(2):
        both = dot(table_ref[r], field)
        total = (both[:, :pair] + sign * both[:, pair:]) * (scale if r == 0 else -scale)
        total = total.astype(BF)
        for s in range(2):
            chosen = (iota((ranks, orders), 1) == order_ref[:, s : s + 1]).astype(BF)
            placed = dot(chosen, total)
            for k in range(lat_dev):
                row = s * 4 + r * 2 + k
                msg_ref[pl.ds(row, ranks, stride=8), :] = placed[:, k * width : (k + 1) * width]
    sent_ref[...] = msg_ref[...].reshape(ranks, 8, width).astype(BF)


def legendre_kernel(
    got_ref, up_ref, down_ref, weight_ref, saved_ref, gain_ref, first_ref, second_ref, msg_ref, out_ref
):
    ranks, rows, width = got_ref.shape
    msg_ref[...] = got_ref[...].astype(F32).reshape(ranks * rows, width)
    gain_real = gain_ref[0]
    gain_imag = gain_ref[1]
    terms = [None, None]
    for s in range(2):
        parts = []
        for r in range(2):
            lanes = [
                msg_ref[pl.ds(s * 4 + r * 2 + k, ranks, stride=8), :].astype(BF) for k in range(2)
            ]
            parts.append(jnp.concatenate(lanes, axis=0))
        found = dot(up_ref[s], jnp.concatenate(parts, axis=1))
        real = found[:, :width]
        imag = found[:, width:]
        saved_real = saved_ref[s, 0].astype(F32)
        saved_imag = saved_ref[s, 1].astype(F32)
        new = (real * saved_real + imag * saved_imag, imag * saved_real - real * saved_imag)
        terms = [n if t is None else t + n for t, n in zip(terms, new)]
        coeff = jnp.concatenate(
            [gain_real * real + gain_imag * imag, gain_real * imag - gain_imag * real], axis=1
        ).astype(BF)
        lat_grad = dot(down_ref[s], coeff)
        for r in range(2):
            weighted = lat_grad[:, r * width : (r + 1) * width] * weight_ref[...]
            for k in range(2):
                out_ref[s, pl.ds(r * 2 + k, ranks, stride=8), :] = weighted[
                    k * ranks : (k + 1) * ranks
                ]
    for g in range(2):
        for h in range(2):
            part = terms[g][h * ranks : (h + 1) * ranks]
            for s in range(2):
                out_ref[s, pl.ds(4 + g * 2 + h, ranks, stride=8), :] = part
    first_ref[...] = out_ref[0].reshape(ranks, rows, width).astype(BF)
    second_ref[...] = out_ref[1].reshape(ranks, rows, width).astype(BF)


def share_kernel(got_ref, half_ref, sent_ref):
    ranks, rows, width = got_ref.shape
    part = ranks // 16
    total = got_ref[0:part].astype(F32)
    for i in range(1, 16):
        total = total + got_ref[i * part : (i + 1) * part].astype(F32)
    total = jnp.sum(total, axis=0, keepdims=True).astype(BF)
    sent_ref[...] = jnp.where(iota(got_ref.shape, 1) < 4, half_ref[...], total)


def field_kernel(
    first_ref, second_ref, order_ref, table_ref, grad_ref, out_ref, gain_ref, msg_ref, field_ref, share_ref, sems
):
    lat_dev, lons, width = grad_ref.shape
    ranks = first_ref.shape[0]
    half = lons // 2
    msg_ref[1] = second_ref[...].astype(F32).reshape(msg_ref.shape[1:])
    for g in range(2):
        for h in range(2):
            share_ref[g, h * ranks : (h + 1) * ranks, :] = msg_ref[
                1, pl.ds(4 + g * 2 + h, ranks, stride=8), :
            ]
    copies = [pltpu.make_async_copy(share_ref, gain_ref, sems.at[0])]
    copies[0].start()
    msg_ref[0] = first_ref[...].astype(F32).reshape(msg_ref.shape[1:])
    sign = jnp.where(iota((half, 1), 0) % 2 == 0, 1.0, -1.0)
    chosen = [
        (iota((half, ranks), 0) == order_ref[s : s + 1, :]).astype(BF) for s in range(2)
    ]
    chosen = jnp.concatenate(chosen, axis=1)
    both = []
    for r in range(2):
        parts = []
        for s in range(2):
            lanes = [msg_ref[s, pl.ds(r * 2 + k, ranks, stride=8), :].astype(BF) for k in range(2)]
            parts.append(jnp.concatenate(lanes, axis=1))
        placed = dot(chosen, jnp.concatenate(parts, axis=0))
        both.append(jnp.concatenate([placed, placed * sign], axis=1).astype(BF))
    block = half // 4
    for i in range(4):
        rows = slice(i * block, (i + 1) * block)
        part = dot(table_ref[0, rows, :], both[0]) - dot(table_ref[1, rows, :], both[1])
        part = part * (1.0 / lons)
        for h in range(2):
            span = slice(h * half + i * block, h * half + (i + 1) * block)
            for k in range(lat_dev):
                at = (h * lat_dev + k) * width
                field_ref[k, span, :] = (grad_ref[k, span, :] + part[:, at : at + width]).astype(BF)
            copies.append(
                pltpu.make_async_copy(
                    field_ref.at[:, span, :], out_ref.at[:, span, :], sems.at[len(copies)]
                )
            )
            copies[-1].start()
    for copy in copies:
        copy.wait()


def exchange(message):
    return lax.all_to_all(message, RANKS, split_axis=0, concat_axis=0, tiled=True)


def on_device(
    next_grad,
    pre_act,
    legendre,
    order_slots,
    quad_weights,
    spectral_gain,
    saved_coeffs,
    obs_value,
    obs_lat_frac,
    obs_lon_frac,
    obs_corner,
    obs_channel,
    slot_counts,
):
    lat_dev, lons, width = next_grad.shape
    slot_dev, degrees, lats = legendre.shape
    orders = order_slots.shape[0]
    ranks = lax.axis_size("lat") * lax.axis_size("obs")
    shape = jax.ShapeDtypeStruct

    index = np.arange(orders)
    angle = ((index[:, None] * index[None, :]) % lons).astype(np.float32) * np.float32(
        2.0 * math.pi / lons
    )
    table = jnp.asarray(np.stack([np.cos(angle), np.sin(angle)]).astype(jnp.bfloat16))

    base = (lax.axis_index("chan") * width).astype(jnp.int32).reshape(1)
    slot_args = (
        obs_value[0],
        obs_lat_frac[0],
        obs_lon_frac[0],
        obs_corner[0],
        obs_channel[0],
        slot_counts,
    )
    slots = exchange(
        call(
            pack_kernel,
            shape((ranks, 128), F32),
            scratch=buffers_for(slot_args),
            smem=1,
            far=range(1, 7),
            limit=60,
        )(base, *slot_args)
    )

    ready_args = (legendre, quad_weights.reshape(1, lats))
    ready = (
        shape(legendre.shape, BF),
        shape((slot_dev, lats, degrees), BF),
        shape((lats, 128), F32),
    )
    prepared = call(
        ready_kernel,
        ready,
        scratch=buffers_for(ready_args) + buffers_for(ready),
        far=range(2),
        far_out=True,
        flops=4 * 2 * 512**3,
        limit=60,
    )(*ready_args)
    order_columns = order_slots.reshape(ranks, 2)
    slots, prepared, order_columns, order_rows = lax.optimization_barrier(
        (slots, prepared, order_columns, order_columns.T)
    )
    up_table, down_table, weight = prepared

    message = shape((ranks, 8, width), BF)
    rows = pltpu.VMEM((ranks * 8, width), F32)
    pairs = pltpu.VMEM((2, ranks * 8, width), F32)
    field = shape(next_grad.shape, F32)
    sent, out_grad = call(
        synth_kernel,
        (message, field),
        scratch=[
            pltpu.VMEM(field.shape, F32),
            pltpu.VMEM((lons // 4, 16 * ranks), BF),
            pltpu.VMEM((10 * width, 16 * ranks), BF),
            pltpu.VMEM(field.shape, F32),
            rows,
        ],
        flops=2 * 1024 * 4096 * 512,
        limit=32,
    )(slots, next_grad, pre_act, table, order_columns)
    by_order = exchange(sent)
    first, second = call(
        legendre_kernel, (message, message), scratch=[rows, pairs], flops=2 * 512**3 * 4
    )(by_order, up_table, down_table, weight, saved_coeffs, spectral_gain)
    first = exchange(first)
    second = exchange(call(share_kernel, message)(first, second))
    outs = (shape(next_grad.shape, BF), shape((2, degrees, width), F32))
    return call(
        field_kernel,
        outs,
        scratch=[pairs]
        + [pltpu.VMEM(o.shape, o.dtype) for o in outs]
        + [pltpu.SemaphoreType.DMA((9,))],
        far_out=True,
        flops=2 * 512**3 * 3,
    )(first, second, order_rows, table, out_grad)


def solution(mesh):
    ranks = P(RANKS, None, None)
    in_specs = (
        P(RANKS, None, "chan"),
        P(RANKS, None, "chan"),
        ranks,
        P(),
        P(),
        P(None, None, "chan"),
        P(RANKS, None, None, "chan"),
        ranks,
        ranks,
        ranks,
        ranks,
        ranks,
        P(RANKS, None),
    )
    out_specs = (P(RANKS, None, "chan"), P(None, None, "chan"))
    return jax.shard_map(
        on_device, mesh=mesh, in_specs=in_specs, out_specs=out_specs, check_vma=False
    )
```

```python
import math

import jax
import jax.numpy as jnp
import numpy as np
from jax import lax
from jax.experimental import pallas as pl
from jax.experimental.pallas import tpu as pltpu
from jax.sharding import PartitionSpec as P

BF = jnp.bfloat16
F32 = jnp.float32
NT = (((1,), (1,)), ((), ()))
RANKS = ("lat", "obs")


def dot(left, right):
    return jnp.dot(left, right, preferred_element_type=F32)


def dot_nt(left, right):
    return lax.dot_general(left, right, NT, preferred_element_type=F32)


def call(kernel, out_shape, scratch=(), smem=0, far=(), far_out=False, flops=0, limit=16):
    outs = out_shape if isinstance(out_shape, tuple) else (out_shape,)
    moved = sum(math.prod(o.shape) * o.dtype.itemsize for o in outs)

    def run(*args):
        specs = [
            pl.BlockSpec(
                memory_space=pltpu.SMEM if i < smem else pltpu.HBM if i in far else pltpu.VMEM
            )
            for i in range(len(args))
        ]
        total = moved + sum(math.prod(a.shape) * a.dtype.itemsize for a in args)
        return pl.pallas_call(
            kernel,
            out_shape=out_shape,
            in_specs=specs,
            out_specs=jax.tree.map(
                lambda _: pl.BlockSpec(memory_space=pltpu.HBM if far_out else pltpu.VMEM), out_shape
            ),
            scratch_shapes=list(scratch),
            compiler_params=pltpu.CompilerParams(vmem_limit_bytes=limit << 20),
            cost_estimate=pl.CostEstimate(flops=flops, bytes_accessed=total, transcendentals=0),
        )(*args)

    return run


def buffers_for(arrays):
    return [pltpu.VMEM(a.shape, a.dtype) for a in arrays] + [pltpu.SemaphoreType.DMA((len(arrays),))]


def start_copies(sources, targets, sems):
    copies = [
        pltpu.make_async_copy(source, target, sems.at[i])
        for i, (source, target) in enumerate(zip(sources, targets))
    ]
    for copy in copies:
        copy.start()
    return copies


def iota(shape, axis):
    return lax.broadcasted_iota(jnp.int32, shape, axis)


def pack_kernel(base_ref, *refs):
    sources, out_ref, buffers, sems = refs[:6], refs[6], refs[7:13], refs[13]
    for copy in start_copies(sources, buffers, sems):
        copy.wait()
    value, lat_frac, lon_frac, corner, chan, counts = [buffer[...] for buffer in buffers]
    capacity, tiles = value.shape
    alive = iota((capacity, tiles), 0) < counts
    fields = [
        jnp.where(alive, value.astype(F32), 0.0),
        lat_frac.astype(F32),
        lon_frac.astype(F32),
        corner.astype(F32),
        (chan - base_ref[0]).astype(F32),
        jnp.zeros((128 - 5 * capacity, tiles), F32),
    ]
    out_ref[...] = jnp.concatenate(fields, axis=0).T


def ready_kernel(far_legendre, far_quad, far_up, far_down, far_weight, legendre_ref, quad_ref, up_ref, down_ref, weight_ref, sems):
    coming = [
        pltpu.make_async_copy(far_legendre.at[0], legendre_ref.at[0], sems.at[0]),
        pltpu.make_async_copy(far_legendre.at[1], legendre_ref.at[1], sems.at[1]),
        pltpu.make_async_copy(far_quad, quad_ref, sems.at[2]),
    ]
    leaving = [pltpu.make_async_copy(weight_ref, far_weight, sems.at[3])]
    for s in range(2):
        leaving.append(pltpu.make_async_copy(up_ref.at[s], far_up.at[s], sems.at[4 + 2 * s]))
        leaving.append(pltpu.make_async_copy(down_ref.at[s], far_down.at[s], sems.at[5 + 2 * s]))
    for copy in coming:
        copy.start()
    lats = legendre_ref.shape[2]
    half = lats // 2
    place = iota((lats, lats), 0)
    chosen = (place % half) * 2 + place // half == iota((lats, lats), 1)
    pick = chosen.astype(BF)
    for s in range(2):
        coming[s].wait()
        up_ref[s] = dot_nt(legendre_ref[s], pick).astype(BF)
        leaving[1 + 2 * s].start()
        down_ref[s] = dot_nt(pick, legendre_ref[s]).astype(BF)
        leaving[2 + 2 * s].start()
    coming[2].wait()
    quad = jnp.sum(jnp.where(chosen, quad_ref[...], 0.0), axis=1, keepdims=True)
    weight_ref[...] = jnp.broadcast_to(quad, weight_ref.shape)
    leaving[0].start()
    for copy in leaving:
        copy.wait()


def tall(row, count):
    block = jnp.broadcast_to(row, (16, row.shape[1])).astype(BF)
    return jnp.concatenate([block] * (count // 16), axis=0)


def synth_kernel(
    slots_ref, next_ref, pre_ref, table_ref, order_ref, sent_ref, grad_ref, slope_ref, rows_ref, cols_ref, field_ref, msg_ref
):
    values = pre_ref[...].astype(F32)
    cdf = 0.5 * (1.0 + lax.erf(values * 0.7071067811865476))
    density = jnp.exp(-0.5 * values * values) * 0.3989422804014327
    slope_ref[...] = cdf + values * density
    lat_dev, lons, width = next_ref.shape
    ranks = slots_ref.shape[0]
    capacity = 16
    groups = lons // 4
    orders = table_ref.shape[1]
    chosen = [
        (iota((ranks, orders), 1) == order_ref[:, s : s + 1]).astype(BF) for s in range(2)
    ]
    chosen = jnp.concatenate(chosen, axis=0)
    fields = slots_ref[...].T
    value = fields[0:16]
    lat_step = fields[16:32]
    lon_step = fields[32:48]
    corner = fields[48:64].astype(jnp.int32)
    chan = fields[64:80]
    group = (corner // 4).astype(F32)
    place = corner % 4
    at_left = ((1.0 - lat_step) * (1.0 - lon_step), lat_step * (1.0 - lon_step))
    at_right = ((1.0 - lat_step) * lon_step, lat_step * lon_step)
    weights = [
        jnp.where(place == j, at_left[k], 0.0) + jnp.where(place == j - 1, at_right[k], 0.0)
        for j in range(5)
        for k in range(lat_dev)
    ]
    chan_ids = iota((width, ranks), 0).astype(F32).astype(BF)
    group_ids = iota((groups, ranks), 0).astype(F32).astype(BF)
    nothing = jnp.zeros((), BF)
    for p in range(capacity):
        span = slice(p * ranks, (p + 1) * ranks)
        rows_ref[:, span] = jnp.where(
            group_ids == tall(group[p : p + 1], groups), tall(value[p : p + 1], groups), nothing
        )
        hit = chan_ids == tall(chan[p : p + 1], width)
        for i, weight in enumerate(weights):
            cols_ref[i * width : (i + 1) * width, span] = jnp.where(
                hit, tall(weight[p : p + 1], width), nothing
            )
    pair = lat_dev * width
    found = [
        dot_nt(rows_ref[...], cols_ref[j * pair : (j + 1) * pair, :]) for j in range(5)
    ]
    found[0] = found[0] + pltpu.roll(found[4], 1, 0)
    for j in range(4):
        for k in range(lat_dev):
            field_ref[k, pl.ds(j, groups, stride=4), :] = found[j][:, k * width : (k + 1) * width]
    halves = []
    for h in range(2):
        at = h * (lons // 2)
        parts = []
        for k in range(lat_dev):
            total = next_ref[k, at : at + lons // 2, :].astype(F32) + field_ref[
                k, at : at + lons // 2, :
            ]
            grad_ref[k, at : at + lons // 2, :] = total
            parts.append((total * slope_ref[k, at : at + lons // 2, :]).astype(BF))
        halves.extend(parts)
    field = jnp.concatenate(halves, axis=1)
    order_ids = iota((orders, 1), 0)
    sign = jnp.where(order_ids % 2 == 0, 1.0, -1.0)
    scale = jnp.where(order_ids == 0, 1.0, 2.0)
    totals = []
    for r in range(2):
        both = dot(table_ref[r], field)
        total = (both[:, :pair] + sign * both[:, pair:]) * (scale if r == 0 else -scale)
        totals.append(total.astype(BF))
    placed = dot(chosen, jnp.concatenate(totals, axis=1))
    for s in range(2):
        for r in range(2):
            for k in range(lat_dev):
                at = r * pair + k * width
                msg_ref[pl.ds(s * 4 + r * 2 + k, ranks, stride=8), :] = placed[
                    s * ranks : (s + 1) * ranks, at : at + width
                ]
    sent_ref[...] = msg_ref[...].reshape(ranks, 8, width).astype(BF)


def legendre_kernel(
    got_ref, up_ref, down_ref, weight_ref, saved_ref, gain_ref, first_ref, second_ref, msg_ref, out_ref
):
    ranks, rows, width = got_ref.shape
    msg_ref[...] = got_ref[...].astype(F32).reshape(ranks * rows, width)
    gain_real = gain_ref[0]
    gain_imag = gain_ref[1]
    terms = [None, None]
    for s in range(2):
        parts = []
        for r in range(2):
            lanes = [
                msg_ref[pl.ds(s * 4 + r * 2 + k, ranks, stride=8), :].astype(BF) for k in range(2)
            ]
            parts.append(jnp.concatenate(lanes, axis=0))
        found = dot(up_ref[s], jnp.concatenate(parts, axis=1))
        real = found[:, :width]
        imag = found[:, width:]
        saved_real = saved_ref[s, 0].astype(F32)
        saved_imag = saved_ref[s, 1].astype(F32)
        new = (real * saved_real + imag * saved_imag, imag * saved_real - real * saved_imag)
        terms = [n if t is None else t + n for t, n in zip(terms, new)]
        coeff = jnp.concatenate(
            [gain_real * real + gain_imag * imag, gain_real * imag - gain_imag * real], axis=1
        ).astype(BF)
        lat_grad = dot(down_ref[s], coeff)
        for r in range(2):
            weighted = lat_grad[:, r * width : (r + 1) * width] * weight_ref[...]
            for k in range(2):
                out_ref[s, pl.ds(r * 2 + k, ranks, stride=8), :] = weighted[
                    k * ranks : (k + 1) * ranks
                ]
    for g in range(2):
        for h in range(2):
            part = terms[g][h * ranks : (h + 1) * ranks]
            for s in range(2):
                out_ref[s, pl.ds(4 + g * 2 + h, ranks, stride=8), :] = part
    first_ref[...] = out_ref[0].reshape(ranks, rows, width).astype(BF)
    second_ref[...] = out_ref[1].reshape(ranks, rows, width).astype(BF)


def share_kernel(got_ref, half_ref, sent_ref):
    ranks, rows, width = got_ref.shape
    part = ranks // 16
    total = got_ref[0:part].astype(F32)
    for i in range(1, 16):
        total = total + got_ref[i * part : (i + 1) * part].astype(F32)
    total = jnp.sum(total, axis=0, keepdims=True).astype(BF)
    sent_ref[...] = jnp.where(iota(got_ref.shape, 1) < 4, half_ref[...], total)


def field_kernel(
    first_ref, second_ref, order_ref, table_ref, grad_ref, out_ref, gain_ref, msg_ref, field_ref, share_ref, sems
):
    lat_dev, lons, width = grad_ref.shape
    ranks = first_ref.shape[0]
    half = lons // 2
    msg_ref[1] = second_ref[...].astype(F32).reshape(msg_ref.shape[1:])
    for g in range(2):
        for h in range(2):
            share_ref[g, h * ranks : (h + 1) * ranks, :] = msg_ref[
                1, pl.ds(4 + g * 2 + h, ranks, stride=8), :
            ]
    copies = [pltpu.make_async_copy(share_ref, gain_ref, sems.at[0])]
    copies[0].start()
    msg_ref[0] = first_ref[...].astype(F32).reshape(msg_ref.shape[1:])
    row = iota((half, ranks), 0)
    order = (row % ranks) * 2 + row // ranks
    chosen = [(order == order_ref[s : s + 1, :]).astype(BF) for s in range(2)]
    chosen = jnp.concatenate(chosen, axis=1)
    placed = []
    for r in range(2):
        parts = []
        for s in range(2):
            lanes = [msg_ref[s, pl.ds(r * 2 + k, ranks, stride=8), :].astype(BF) for k in range(2)]
            parts.append(jnp.concatenate(lanes, axis=1))
        placed.append(dot(chosen, jnp.concatenate(parts, axis=0)).astype(BF))
    even = jnp.concatenate([p[:ranks] for p in placed], axis=0)
    odd = jnp.concatenate([p[ranks:] for p in placed], axis=0)
    block = half // 4
    for i in range(4):
        rows = slice(i * block, (i + 1) * block)
        same = dot(table_ref[0, rows, :], even)
        turned = dot(table_ref[1, rows, :], odd)
        for h in range(2):
            span = slice(h * half + i * block, h * half + (i + 1) * block)
            for k in range(lat_dev):
                lanes = slice(k * width, (k + 1) * width)
                part = same[:, lanes] + turned[:, lanes] if h == 0 else same[:, lanes] - turned[:, lanes]
                field_ref[k, span, :] = (grad_ref[k, span, :] + part).astype(BF)
            copies.append(
                pltpu.make_async_copy(
                    field_ref.at[:, span, :], out_ref.at[:, span, :], sems.at[len(copies)]
                )
            )
            copies[-1].start()
    for copy in copies:
        copy.wait()


def exchange(message):
    return lax.all_to_all(message, RANKS, split_axis=0, concat_axis=0, tiled=True)


def on_device(
    next_grad,
    pre_act,
    legendre,
    order_slots,
    quad_weights,
    spectral_gain,
    saved_coeffs,
    obs_value,
    obs_lat_frac,
    obs_lon_frac,
    obs_corner,
    obs_channel,
    slot_counts,
):
    lat_dev, lons, width = next_grad.shape
    slot_dev, degrees, lats = legendre.shape
    orders = order_slots.shape[0]
    ranks = lax.axis_size("lat") * lax.axis_size("obs")
    shape = jax.ShapeDtypeStruct

    index = np.arange(orders)
    angle = ((index[:, None] * index[None, :]) % lons).astype(np.float32) * np.float32(
        2.0 * math.pi / lons
    )
    waves = np.stack([np.cos(angle), np.sin(angle)]).astype(jnp.bfloat16)
    table = jnp.asarray(waves)
    back = np.stack([waves[0].astype(np.float32), -waves[1].astype(np.float32)]) / lons
    back = [np.concatenate([back[0, :, p::2], back[1, :, p::2]], axis=1) for p in range(2)]
    back = jnp.asarray(np.stack(back).astype(jnp.bfloat16))

    base = (lax.axis_index("chan") * width).astype(jnp.int32).reshape(1)
    slot_args = (
        obs_value[0],
        obs_lat_frac[0],
        obs_lon_frac[0],
        obs_corner[0],
        obs_channel[0],
        slot_counts,
    )
    slots = exchange(
        call(
            pack_kernel,
            shape((ranks, 128), F32),
            scratch=buffers_for(slot_args),
            smem=1,
            far=range(1, 7),
            limit=60,
        )(base, *slot_args)
    )

    ready_args = (legendre, quad_weights.reshape(1, lats))
    ready = (
        shape(legendre.shape, BF),
        shape((slot_dev, lats, degrees), BF),
        shape((lats, 128), F32),
    )
    prepared = call(
        ready_kernel,
        ready,
        scratch=buffers_for(ready_args)[:-1]
        + buffers_for(ready)[:-1]
        + [pltpu.SemaphoreType.DMA((8,))],
        far=range(2),
        far_out=True,
        flops=4 * 2 * 512**3,
        limit=60,
    )(*ready_args)
    order_columns = order_slots.reshape(ranks, 2)
    slots, prepared, order_columns, order_rows = lax.optimization_barrier(
        (slots, prepared, order_columns, order_columns.T)
    )
    up_table, down_table, weight = prepared

    message = shape((ranks, 8, width), BF)
    rows = pltpu.VMEM((ranks * 8, width), F32)
    pairs = pltpu.VMEM((2, ranks * 8, width), F32)
    field = shape(next_grad.shape, F32)
    sent, out_grad = call(
        synth_kernel,
        (message, field),
        scratch=[
            pltpu.VMEM(field.shape, F32),
            pltpu.VMEM((lons // 4, 16 * ranks), BF),
            pltpu.VMEM((10 * width, 16 * ranks), BF),
            pltpu.VMEM(field.shape, F32),
            rows,
        ],
        flops=2 * 1024 * 4096 * 512,
        limit=32,
    )(slots, next_grad, pre_act, table, order_columns)
    by_order = exchange(sent)
    first, second = call(
        legendre_kernel, (message, message), scratch=[rows, pairs], flops=2 * 512**3 * 4
    )(by_order, up_table, down_table, weight, saved_coeffs, spectral_gain)
    first = exchange(first)
    second = exchange(call(share_kernel, message)(first, second))
    outs = (shape(next_grad.shape, BF), shape((2, degrees, width), F32))
    return call(
        field_kernel,
        outs,
        scratch=[pairs]
        + [pltpu.VMEM(o.shape, o.dtype) for o in outs]
        + [pltpu.SemaphoreType.DMA((9,))],
        far_out=True,
        flops=2 * 512**3 * 3,
    )(first, second, order_rows, back, out_grad)


def solution(mesh):
    ranks = P(RANKS, None, None)
    in_specs = (
        P(RANKS, None, "chan"),
        P(RANKS, None, "chan"),
        ranks,
        P(),
        P(),
        P(None, None, "chan"),
        P(RANKS, None, None, "chan"),
        ranks,
        ranks,
        ranks,
        ranks,
        ranks,
        P(RANKS, None),
    )
    out_specs = (P(RANKS, None, "chan"), P(None, None, "chan"))
    return jax.shard_map(
        on_device, mesh=mesh, in_specs=in_specs, out_specs=out_specs, check_vma=False
    )
```

```python
import math

import jax
import jax.numpy as jnp
import numpy as np
from jax import lax
from jax.experimental import pallas as pl
from jax.experimental.pallas import tpu as pltpu
from jax.sharding import PartitionSpec as P

BF = jnp.bfloat16
F32 = jnp.float32
NT = (((1,), (1,)), ((), ()))
RANKS = ("lat", "obs")


def dot(left, right):
    return jnp.dot(left, right, preferred_element_type=F32)


def dot_nt(left, right):
    return lax.dot_general(left, right, NT, preferred_element_type=F32)


def call(kernel, out_shape, scratch=(), smem=0, far=(), far_out=False, aliases=None, flops=0, limit=16):
    outs = out_shape if isinstance(out_shape, tuple) else (out_shape,)
    moved = sum(math.prod(o.shape) * o.dtype.itemsize for o in outs)

    def run(*args):
        specs = [
            pl.BlockSpec(
                memory_space=pltpu.SMEM if i < smem else pltpu.HBM if i in far else pltpu.VMEM
            )
            for i in range(len(args))
        ]
        total = moved + sum(math.prod(a.shape) * a.dtype.itemsize for a in args)
        return pl.pallas_call(
            kernel,
            out_shape=out_shape,
            in_specs=specs,
            out_specs=jax.tree.map(
                lambda _: pl.BlockSpec(memory_space=pltpu.HBM if far_out else pltpu.VMEM), out_shape
            ),
            scratch_shapes=list(scratch),
            input_output_aliases=aliases or {},
            compiler_params=pltpu.CompilerParams(vmem_limit_bytes=limit << 20),
            cost_estimate=pl.CostEstimate(flops=flops, bytes_accessed=total, transcendentals=0),
        )(*args)

    return run


def buffers_for(arrays):
    return [pltpu.VMEM(a.shape, a.dtype) for a in arrays] + [pltpu.SemaphoreType.DMA((len(arrays),))]


def start_copies(sources, targets, sems):
    copies = [
        pltpu.make_async_copy(source, target, sems.at[i])
        for i, (source, target) in enumerate(zip(sources, targets))
    ]
    for copy in copies:
        copy.start()
    return copies


def iota(shape, axis):
    return lax.broadcasted_iota(jnp.int32, shape, axis)


def pack_kernel(base_ref, *refs):
    sources, out_ref, buffers, sems = refs[:6], refs[6], refs[7:13], refs[13]
    for copy in start_copies(sources, buffers, sems):
        copy.wait()
    value, lat_frac, lon_frac, corner, chan, counts = [buffer[...] for buffer in buffers]
    capacity, tiles = value.shape
    alive = iota((capacity, tiles), 0) < counts
    fields = [
        jnp.where(alive, value.astype(F32), 0.0),
        lat_frac.astype(F32),
        lon_frac.astype(F32),
        corner.astype(F32),
        (chan - base_ref[0]).astype(F32),
        jnp.zeros((128 - 5 * capacity, tiles), F32),
    ]
    out_ref[...] = jnp.concatenate(fields, axis=0).T


def ready_kernel(turn_ref, far_legendre, far_quad, *refs):
    far_up, far_down, far_weight, legendre_ref, quad_ref, up_ref, down_ref, weight_ref, sems = refs[-9:]

    @pl.when(turn_ref[0] == 1)
    def _():
        coming = [
            pltpu.make_async_copy(far_legendre.at[0], legendre_ref.at[0], sems.at[0]),
            pltpu.make_async_copy(far_legendre.at[1], legendre_ref.at[1], sems.at[1]),
            pltpu.make_async_copy(far_quad, quad_ref, sems.at[2]),
        ]
        leaving = [pltpu.make_async_copy(weight_ref, far_weight, sems.at[3])]
        for s in range(2):
            leaving.append(pltpu.make_async_copy(up_ref.at[s], far_up.at[s], sems.at[4 + 2 * s]))
            leaving.append(pltpu.make_async_copy(down_ref.at[s], far_down.at[s], sems.at[5 + 2 * s]))
        for copy in coming:
            copy.start()
        lats = legendre_ref.shape[2]
        half = lats // 2
        place = iota((lats, lats), 0)
        chosen = (place % half) * 2 + place // half == iota((lats, lats), 1)
        pick = chosen.astype(BF)
        for s in range(2):
            coming[s].wait()
            up_ref[s] = dot_nt(legendre_ref[s], pick).astype(BF)
            leaving[1 + 2 * s].start()
            down_ref[s] = dot_nt(pick, legendre_ref[s]).astype(BF)
            leaving[2 + 2 * s].start()
        coming[2].wait()
        quad = jnp.sum(jnp.where(chosen, quad_ref[...], 0.0), axis=1, keepdims=True)
        weight_ref[...] = jnp.broadcast_to(quad, weight_ref.shape)
        leaving[0].start()
        for copy in leaving:
            copy.wait()


def tall(row, count):
    block = jnp.broadcast_to(row, (16, row.shape[1])).astype(BF)
    return jnp.concatenate([block] * (count // 16), axis=0)


def synth_kernel(
    slots_ref, next_ref, pre_ref, table_ref, order_ref, sent_ref, grad_ref, slope_ref, rows_ref, cols_ref, field_ref, msg_ref
):
    values = pre_ref[...].astype(F32)
    cdf = 0.5 * (1.0 + lax.erf(values * 0.7071067811865476))
    density = jnp.exp(-0.5 * values * values) * 0.3989422804014327
    slope_ref[...] = cdf + values * density
    lat_dev, lons, width = next_ref.shape
    ranks = slots_ref.shape[0]
    capacity = 16
    groups = lons // 4
    orders = table_ref.shape[1]
    chosen = [
        (iota((ranks, orders), 1) == order_ref[:, s : s + 1]).astype(BF) for s in range(2)
    ]
    chosen = jnp.concatenate(chosen, axis=0)
    fields = slots_ref[...].T
    value = fields[0:16]
    lat_step = fields[16:32]
    lon_step = fields[32:48]
    corner = fields[48:64].astype(jnp.int32)
    chan = fields[64:80]
    group = (corner // 4).astype(F32)
    place = corner % 4
    at_left = ((1.0 - lat_step) * (1.0 - lon_step), lat_step * (1.0 - lon_step))
    at_right = ((1.0 - lat_step) * lon_step, lat_step * lon_step)
    weights = [
        jnp.where(place == j, at_left[k], 0.0) + jnp.where(place == j - 1, at_right[k], 0.0)
        for j in range(5)
        for k in range(lat_dev)
    ]
    chan_ids = iota((width, ranks), 0).astype(F32).astype(BF)
    group_ids = iota((groups, ranks), 0).astype(F32).astype(BF)
    nothing = jnp.zeros((), BF)
    for p in range(capacity):
        span = slice(p * ranks, (p + 1) * ranks)
        rows_ref[:, span] = jnp.where(
            group_ids == tall(group[p : p + 1], groups), tall(value[p : p + 1], groups), nothing
        )
        hit = chan_ids == tall(chan[p : p + 1], width)
        for i, weight in enumerate(weights):
            cols_ref[i * width : (i + 1) * width, span] = jnp.where(
                hit, tall(weight[p : p + 1], width), nothing
            )
    pair = lat_dev * width
    found = [
        dot_nt(rows_ref[...], cols_ref[j * pair : (j + 1) * pair, :]) for j in range(5)
    ]
    found[0] = found[0] + pltpu.roll(found[4], 1, 0)
    for j in range(4):
        for k in range(lat_dev):
            field_ref[k, pl.ds(j, groups, stride=4), :] = found[j][:, k * width : (k + 1) * width]
    halves = []
    for h in range(2):
        at = h * (lons // 2)
        parts = []
        for k in range(lat_dev):
            total = next_ref[k, at : at + lons // 2, :].astype(F32) + field_ref[
                k, at : at + lons // 2, :
            ]
            grad_ref[k, at : at + lons // 2, :] = total
            parts.append((total * slope_ref[k, at : at + lons // 2, :]).astype(BF))
        halves.extend(parts)
    field = jnp.concatenate(halves, axis=1)
    order_ids = iota((orders, 1), 0)
    sign = jnp.where(order_ids % 2 == 0, 1.0, -1.0)
    scale = jnp.where(order_ids == 0, 1.0, 2.0)
    totals = []
    for r in range(2):
        both = dot(table_ref[r], field)
        total = (both[:, :pair] + sign * both[:, pair:]) * (scale if r == 0 else -scale)
        totals.append(total.astype(BF))
    placed = dot(chosen, jnp.concatenate(totals, axis=1))
    for s in range(2):
        for r in range(2):
            for k in range(lat_dev):
                at = r * pair + k * width
                msg_ref[pl.ds(s * 4 + r * 2 + k, ranks, stride=8), :] = placed[
                    s * ranks : (s + 1) * ranks, at : at + width
                ]
    sent_ref[...] = msg_ref[...].reshape(ranks, 8, width).astype(BF)


def legendre_kernel(
    got_ref, up_ref, down_ref, weight_ref, saved_ref, gain_ref, first_ref, second_ref, msg_ref, out_ref
):
    ranks, rows, width = got_ref.shape
    msg_ref[...] = got_ref[...].astype(F32).reshape(ranks * rows, width)
    gain_real = gain_ref[0]
    gain_imag = gain_ref[1]
    terms = [None, None]
    for s in range(2):
        parts = []
        for r in range(2):
            lanes = [
                msg_ref[pl.ds(s * 4 + r * 2 + k, ranks, stride=8), :].astype(BF) for k in range(2)
            ]
            parts.append(jnp.concatenate(lanes, axis=0))
        found = dot(up_ref[s], jnp.concatenate(parts, axis=1))
        real = found[:, :width]
        imag = found[:, width:]
        saved_real = saved_ref[s, 0].astype(F32)
        saved_imag = saved_ref[s, 1].astype(F32)
        new = (real * saved_real + imag * saved_imag, imag * saved_real - real * saved_imag)
        terms = [n if t is None else t + n for t, n in zip(terms, new)]
        coeff = jnp.concatenate(
            [gain_real * real + gain_imag * imag, gain_real * imag - gain_imag * real], axis=1
        ).astype(BF)
        lat_grad = dot(down_ref[s], coeff)
        for r in range(2):
            weighted = lat_grad[:, r * width : (r + 1) * width] * weight_ref[...]
            for k in range(2):
                out_ref[s, pl.ds(r * 2 + k, ranks, stride=8), :] = weighted[
                    k * ranks : (k + 1) * ranks
                ]
    for g in range(2):
        for h in range(2):
            part = terms[g][h * ranks : (h + 1) * ranks]
            for s in range(2):
                out_ref[s, pl.ds(4 + g * 2 + h, ranks, stride=8), :] = part
    first_ref[...] = out_ref[0].reshape(ranks, rows, width).astype(BF)
    second_ref[...] = out_ref[1].reshape(ranks, rows, width).astype(BF)


def share_kernel(got_ref, half_ref, sent_ref):
    ranks, rows, width = got_ref.shape
    part = ranks // 16
    total = got_ref[0:part].astype(F32)
    for i in range(1, 16):
        total = total + got_ref[i * part : (i + 1) * part].astype(F32)
    total = jnp.sum(total, axis=0, keepdims=True).astype(BF)
    sent_ref[...] = jnp.where(iota(got_ref.shape, 1) < 4, half_ref[...], total)


def field_kernel(
    first_ref, second_ref, order_ref, table_ref, grad_ref, out_ref, gain_ref, msg_ref, field_ref, share_ref, sems
):
    lat_dev, lons, width = grad_ref.shape
    ranks = first_ref.shape[0]
    half = lons // 2
    msg_ref[1] = second_ref[...].astype(F32).reshape(msg_ref.shape[1:])
    for g in range(2):
        for h in range(2):
            share_ref[g, h * ranks : (h + 1) * ranks, :] = msg_ref[
                1, pl.ds(4 + g * 2 + h, ranks, stride=8), :
            ]
    copies = [pltpu.make_async_copy(share_ref, gain_ref, sems.at[0])]
    copies[0].start()
    msg_ref[0] = first_ref[...].astype(F32).reshape(msg_ref.shape[1:])
    row = iota((half, ranks), 0)
    order = (row % ranks) * 2 + row // ranks
    chosen = [(order == order_ref[s : s + 1, :]).astype(BF) for s in range(2)]
    chosen = jnp.concatenate(chosen, axis=1)
    placed = []
    for r in range(2):
        parts = []
        for s in range(2):
            lanes = [msg_ref[s, pl.ds(r * 2 + k, ranks, stride=8), :].astype(BF) for k in range(2)]
            parts.append(jnp.concatenate(lanes, axis=1))
        placed.append(dot(chosen, jnp.concatenate(parts, axis=0)).astype(BF))
    even = jnp.concatenate([p[:ranks] for p in placed], axis=0)
    odd = jnp.concatenate([p[ranks:] for p in placed], axis=0)
    block = half // 4
    for i in range(4):
        rows = slice(i * block, (i + 1) * block)
        same = dot(table_ref[0, rows, :], even)
        turned = dot(table_ref[1, rows, :], odd)
        for h in range(2):
            span = slice(h * half + i * block, h * half + (i + 1) * block)
            for k in range(lat_dev):
                lanes = slice(k * width, (k + 1) * width)
                part = same[:, lanes] + turned[:, lanes] if h == 0 else same[:, lanes] - turned[:, lanes]
                field_ref[k, span, :] = (grad_ref[k, span, :] + part).astype(BF)
            copies.append(
                pltpu.make_async_copy(
                    field_ref.at[:, span, :], out_ref.at[:, span, :], sems.at[len(copies)]
                )
            )
            copies[-1].start()
    for copy in copies:
        copy.wait()


def exchange(message):
    return lax.all_to_all(message, RANKS, split_axis=0, concat_axis=0, tiled=True)


def on_device(
    next_grad,
    pre_act,
    legendre,
    order_slots,
    quad_weights,
    spectral_gain,
    saved_coeffs,
    obs_value,
    obs_lat_frac,
    obs_lon_frac,
    obs_corner,
    obs_channel,
    slot_counts,
):
    lat_dev, lons, width = next_grad.shape
    slot_dev, degrees, lats = legendre.shape
    orders = order_slots.shape[0]
    ranks = lax.axis_size("lat") * lax.axis_size("obs")
    shape = jax.ShapeDtypeStruct

    index = np.arange(orders)
    angle = ((index[:, None] * index[None, :]) % lons).astype(np.float32) * np.float32(
        2.0 * math.pi / lons
    )
    waves = np.stack([np.cos(angle), np.sin(angle)]).astype(jnp.bfloat16)
    table = jnp.asarray(waves)
    back = np.stack([waves[0].astype(np.float32), -waves[1].astype(np.float32)]) / lons
    back = [np.concatenate([back[0, :, p::2], back[1, :, p::2]], axis=1) for p in range(2)]
    back = jnp.asarray(np.stack(back).astype(jnp.bfloat16))

    core = lax.axis_index("chan").astype(jnp.int32).reshape(1)
    slot_args = (
        obs_value[0],
        obs_lat_frac[0],
        obs_lon_frac[0],
        obs_corner[0],
        obs_channel[0],
        slot_counts,
    )
    packed = call(
        pack_kernel,
        shape((ranks, 128), F32),
        scratch=buffers_for(slot_args),
        smem=1,
        far=range(1, 7),
        limit=60,
    )(core * width, *slot_args)

    ready_args = (legendre, quad_weights.reshape(1, lats))
    ready = (
        shape(legendre.shape, BF),
        shape((slot_dev, lats, degrees), BF),
        shape((lats, 128), F32),
    )

    def prepare(turn, before=()):
        return call(
            ready_kernel,
            ready,
            scratch=buffers_for(ready_args)[:-1]
            + buffers_for(ready)[:-1]
            + [pltpu.SemaphoreType.DMA((8,))],
            smem=1,
            far=range(1, 6),
            far_out=True,
            aliases={3 + i: i for i in range(len(before))},
            flops=4 * 2 * 512**3,
            limit=60,
        )(turn, *ready_args, *before)

    packed, prepared = lax.optimization_barrier((packed, prepare(1 - core)))
    slots = exchange(packed)
    prepared = prepare(core, prepared)
    order_columns = order_slots.reshape(ranks, 2)
    slots, prepared, order_columns, order_rows = lax.optimization_barrier(
        (slots, prepared, order_columns, order_columns.T)
    )
    up_table, down_table, weight = prepared

    message = shape((ranks, 8, width), BF)
    rows = pltpu.VMEM((ranks * 8, width), F32)
    pairs = pltpu.VMEM((2, ranks * 8, width), F32)
    field = shape(next_grad.shape, F32)
    sent, out_grad = call(
        synth_kernel,
        (message, field),
        scratch=[
            pltpu.VMEM(field.shape, F32),
            pltpu.VMEM((lons // 4, 16 * ranks), BF),
            pltpu.VMEM((10 * width, 16 * ranks), BF),
            pltpu.VMEM(field.shape, F32),
            rows,
        ],
        flops=2 * 1024 * 4096 * 512,
        limit=32,
    )(slots, next_grad, pre_act, table, order_columns)
    by_order = exchange(sent)
    first, second = call(
        legendre_kernel, (message, message), scratch=[rows, pairs], flops=2 * 512**3 * 4
    )(by_order, up_table, down_table, weight, saved_coeffs, spectral_gain)
    first = exchange(first)
    second = exchange(call(share_kernel, message)(first, second))
    outs = (shape(next_grad.shape, BF), shape((2, degrees, width), F32))
    return call(
        field_kernel,
        outs,
        scratch=[pairs]
        + [pltpu.VMEM(o.shape, o.dtype) for o in outs]
        + [pltpu.SemaphoreType.DMA((9,))],
        far_out=True,
        flops=2 * 512**3 * 3,
    )(first, second, order_rows, back, out_grad)


def solution(mesh):
    ranks = P(RANKS, None, None)
    in_specs = (
        P(RANKS, None, "chan"),
        P(RANKS, None, "chan"),
        ranks,
        P(),
        P(),
        P(None, None, "chan"),
        P(RANKS, None, None, "chan"),
        ranks,
        ranks,
        ranks,
        ranks,
        ranks,
        P(RANKS, None),
    )
    out_specs = (P(RANKS, None, "chan"), P(None, None, "chan"))
    return jax.shard_map(
        on_device, mesh=mesh, in_specs=in_specs, out_specs=out_specs, check_vma=False
    )
```

```python
import math

import jax
import jax.numpy as jnp
import numpy as np
from jax import lax
from jax.experimental import pallas as pl
from jax.experimental.pallas import tpu as pltpu
from jax.sharding import PartitionSpec as P

BF = jnp.bfloat16
F32 = jnp.float32
NT = (((1,), (1,)), ((), ()))
RANKS = ("lat", "obs")


def dot(left, right):
    return jnp.dot(left, right, preferred_element_type=F32)


def dot_nt(left, right):
    return lax.dot_general(left, right, NT, preferred_element_type=F32)


def call(kernel, out_shape, scratch=(), smem=0, far=(), far_out=False, aliases=None, flops=0, limit=16):
    outs = out_shape if isinstance(out_shape, tuple) else (out_shape,)
    moved = sum(math.prod(o.shape) * o.dtype.itemsize for o in outs)

    def run(*args):
        specs = [
            pl.BlockSpec(
                memory_space=pltpu.SMEM if i < smem else pltpu.HBM if i in far else pltpu.VMEM
            )
            for i in range(len(args))
        ]
        total = moved + sum(math.prod(a.shape) * a.dtype.itemsize for a in args)
        return pl.pallas_call(
            kernel,
            out_shape=out_shape,
            in_specs=specs,
            out_specs=jax.tree.map(
                lambda _: pl.BlockSpec(memory_space=pltpu.HBM if far_out else pltpu.VMEM), out_shape
            ),
            scratch_shapes=list(scratch),
            input_output_aliases=aliases or {},
            compiler_params=pltpu.CompilerParams(vmem_limit_bytes=limit << 20),
            cost_estimate=pl.CostEstimate(flops=flops, bytes_accessed=total, transcendentals=0),
        )(*args)

    return run


def buffers_for(arrays):
    return [pltpu.VMEM(a.shape, a.dtype) for a in arrays] + [pltpu.SemaphoreType.DMA((len(arrays),))]


def start_copies(sources, targets, sems):
    copies = [
        pltpu.make_async_copy(source, target, sems.at[i])
        for i, (source, target) in enumerate(zip(sources, targets))
    ]
    for copy in copies:
        copy.start()
    return copies


def iota(shape, axis):
    return lax.broadcasted_iota(jnp.int32, shape, axis)


def pack_kernel(base_ref, *refs):
    sources, out_ref, buffers, sems = refs[:6], refs[6], refs[7:13], refs[13]
    for copy in start_copies(sources, buffers, sems):
        copy.wait()
    value, lat_frac, lon_frac, corner, chan, counts = [buffer[...] for buffer in buffers]
    capacity, tiles = value.shape
    alive = iota((capacity, tiles), 0) < counts
    fields = [
        jnp.where(alive, value.astype(F32), 0.0),
        lat_frac.astype(F32),
        lon_frac.astype(F32),
        corner.astype(F32),
        (chan - base_ref[0]).astype(F32),
        jnp.zeros((128 - 5 * capacity, tiles), F32),
    ]
    out_ref[...] = jnp.concatenate(fields, axis=0).T


def ready_kernel(turn_ref, far_legendre, far_quad, *refs):
    far_up, far_down, far_weight, legendre_ref, quad_ref, up_ref, down_ref, weight_ref, sems = refs[-9:]

    @pl.when(turn_ref[0] == 1)
    def _():
        coming = [
            pltpu.make_async_copy(far_legendre.at[0], legendre_ref.at[0], sems.at[0]),
            pltpu.make_async_copy(far_legendre.at[1], legendre_ref.at[1], sems.at[1]),
            pltpu.make_async_copy(far_quad, quad_ref, sems.at[2]),
        ]
        leaving = [pltpu.make_async_copy(weight_ref, far_weight, sems.at[3])]
        for s in range(2):
            leaving.append(pltpu.make_async_copy(up_ref.at[s], far_up.at[s], sems.at[4 + 2 * s]))
            leaving.append(pltpu.make_async_copy(down_ref.at[s], far_down.at[s], sems.at[5 + 2 * s]))
        for copy in coming:
            copy.start()
        lats = legendre_ref.shape[2]
        half = lats // 2
        place = iota((lats, lats), 0)
        chosen = (place % half) * 2 + place // half == iota((lats, lats), 1)
        pick = chosen.astype(BF)
        for s in range(2):
            coming[s].wait()
            up_ref[s] = dot_nt(legendre_ref[s], pick).astype(BF)
            leaving[1 + 2 * s].start()
            down_ref[s] = dot_nt(pick, legendre_ref[s]).astype(BF)
            leaving[2 + 2 * s].start()
        coming[2].wait()
        quad = jnp.sum(jnp.where(chosen, quad_ref[...], 0.0), axis=1, keepdims=True)
        weight_ref[...] = jnp.broadcast_to(quad, weight_ref.shape)
        leaving[0].start()
        for copy in leaving:
            copy.wait()


def early_kernel(turn_ref, far_order, far_table, far_out, order_ref, table_ref, out_ref, sems):
    @pl.when(turn_ref[0] == 1)
    def _():
        coming = start_copies((far_order, far_table), (order_ref, table_ref), sems)
        coming[0].wait()
        orders = table_ref.shape[1]
        half = orders // 2
        place = iota((orders, orders), 0)
        chosen = (place % half) * 2 + place // half == iota((orders, orders), 1)
        order = jnp.where(chosen, order_ref[...].astype(F32), 0.0)
        order = jnp.sum(order, axis=1, keepdims=True).astype(jnp.int32)
        scale = jnp.where(order == 0, 1.0, 2.0)
        chosen = (iota((orders, orders), 1) == order).astype(BF)
        coming[1].wait()
        for r in range(2):
            out_ref[r] = (dot(chosen, table_ref[r]) * (scale if r == 0 else -scale)).astype(BF)
        for copy in start_copies((out_ref,), (far_out,), sems):
            copy.wait()


def tall(row, count):
    block = jnp.broadcast_to(row, (16, row.shape[1])).astype(BF)
    return jnp.concatenate([block] * (count // 16), axis=0)


def synth_kernel(
    core_ref,
    slots_ref,
    next_ref,
    pre_ref,
    table_ref,
    early_ref,
    order_ref,
    sent_ref,
    grad_ref,
    slope_ref,
    rows_ref,
    cols_ref,
    field_ref,
    halves_ref,
    msg_ref,
):
    values = pre_ref[...].astype(F32)
    cdf = 0.5 * (1.0 + lax.erf(values * 0.7071067811865476))
    density = jnp.exp(-0.5 * values * values) * 0.3989422804014327
    slope_ref[...] = cdf + values * density
    lat_dev, lons, width = next_ref.shape
    ranks = slots_ref.shape[0]
    capacity = 16
    groups = lons // 4
    orders = table_ref.shape[1]
    fields = slots_ref[...].T
    value = fields[0:16]
    lat_step = fields[16:32]
    lon_step = fields[32:48]
    corner = fields[48:64].astype(jnp.int32)
    chan = fields[64:80]
    group = (corner // 4).astype(F32)
    place = corner % 4
    at_left = ((1.0 - lat_step) * (1.0 - lon_step), lat_step * (1.0 - lon_step))
    at_right = ((1.0 - lat_step) * lon_step, lat_step * lon_step)
    weights = [
        jnp.where(place == j, at_left[k], 0.0) + jnp.where(place == j - 1, at_right[k], 0.0)
        for j in range(5)
        for k in range(lat_dev)
    ]
    chan_ids = iota((width, ranks), 0).astype(F32).astype(BF)
    group_ids = iota((groups, ranks), 0).astype(F32).astype(BF)
    nothing = jnp.zeros((), BF)
    for p in range(capacity):
        span = slice(p * ranks, (p + 1) * ranks)
        rows_ref[:, span] = jnp.where(
            group_ids == tall(group[p : p + 1], groups), tall(value[p : p + 1], groups), nothing
        )
        hit = chan_ids == tall(chan[p : p + 1], width)
        for i, weight in enumerate(weights):
            cols_ref[i * width : (i + 1) * width, span] = jnp.where(
                hit, tall(weight[p : p + 1], width), nothing
            )
    pair = lat_dev * width
    found = [
        dot_nt(rows_ref[...], cols_ref[j * pair : (j + 1) * pair, :]) for j in range(5)
    ]
    found[0] = found[0] + pltpu.roll(found[4], 1, 0)
    for j in range(4):
        for k in range(lat_dev):
            field_ref[k, pl.ds(j, groups, stride=4), :] = found[j][:, k * width : (k + 1) * width]
    halves = []
    for h in range(2):
        at = h * (lons // 2)
        parts = []
        for k in range(lat_dev):
            total = next_ref[k, at : at + lons // 2, :].astype(F32) + field_ref[
                k, at : at + lons // 2, :
            ]
            grad_ref[k, at : at + lons // 2, :] = total
            parts.append((total * slope_ref[k, at : at + lons // 2, :]).astype(BF))
        halves.extend(parts)
    halves_ref[...] = jnp.concatenate(halves, axis=1)

    def store(total, r):
        for s in range(2):
            for k in range(lat_dev):
                msg_ref[pl.ds(s * 4 + r * 2 + k, ranks, stride=8), :] = total[
                    s * ranks : (s + 1) * ranks, k * width : (k + 1) * width
                ]

    @pl.when(core_ref[0] == 0)
    def _():
        order = jnp.concatenate([order_ref[:, s : s + 1] for s in range(2)], axis=0)
        sign = jnp.where(order % 2 == 0, 1.0, -1.0)
        for r in range(2):
            both = dot(early_ref[r], halves_ref[...])
            store(both[:, :pair] + sign * both[:, pair:], r)

    @pl.when(core_ref[0] == 1)
    def _():
        chosen = [
            (iota((ranks, orders), 1) == order_ref[:, s : s + 1]).astype(BF) for s in range(2)
        ]
        chosen = jnp.concatenate(chosen, axis=0)
        order_ids = iota((orders, 1), 0)
        sign = jnp.where(order_ids % 2 == 0, 1.0, -1.0)
        scale = jnp.where(order_ids == 0, 1.0, 2.0)
        totals = []
        for r in range(2):
            both = dot(table_ref[r], halves_ref[...])
            total = (both[:, :pair] + sign * both[:, pair:]) * (scale if r == 0 else -scale)
            totals.append(total.astype(BF))
        placed = dot(chosen, jnp.concatenate(totals, axis=1))
        for r in range(2):
            store(placed[:, r * pair : (r + 1) * pair], r)

    sent_ref[...] = msg_ref[...].reshape(ranks, 8, width).astype(BF)


def legendre_kernel(
    got_ref, up_ref, down_ref, weight_ref, saved_ref, gain_ref, first_ref, second_ref, msg_ref, out_ref
):
    ranks, rows, width = got_ref.shape
    msg_ref[...] = got_ref[...].astype(F32).reshape(ranks * rows, width)
    gain_real = gain_ref[0]
    gain_imag = gain_ref[1]
    terms = [None, None]
    for s in range(2):
        parts = []
        for r in range(2):
            lanes = [
                msg_ref[pl.ds(s * 4 + r * 2 + k, ranks, stride=8), :].astype(BF) for k in range(2)
            ]
            parts.append(jnp.concatenate(lanes, axis=0))
        found = dot(up_ref[s], jnp.concatenate(parts, axis=1))
        real = found[:, :width]
        imag = found[:, width:]
        saved_real = saved_ref[s, 0].astype(F32)
        saved_imag = saved_ref[s, 1].astype(F32)
        new = (real * saved_real + imag * saved_imag, imag * saved_real - real * saved_imag)
        terms = [n if t is None else t + n for t, n in zip(terms, new)]
        coeff = jnp.concatenate(
            [gain_real * real + gain_imag * imag, gain_real * imag - gain_imag * real], axis=1
        ).astype(BF)
        lat_grad = dot(down_ref[s], coeff)
        for r in range(2):
            weighted = lat_grad[:, r * width : (r + 1) * width] * weight_ref[...]
            for k in range(2):
                out_ref[s, pl.ds(r * 2 + k, ranks, stride=8), :] = weighted[
                    k * ranks : (k + 1) * ranks
                ]
    for g in range(2):
        for h in range(2):
            part = terms[g][h * ranks : (h + 1) * ranks]
            for s in range(2):
                out_ref[s, pl.ds(4 + g * 2 + h, ranks, stride=8), :] = part
    first_ref[...] = out_ref[0].reshape(ranks, rows, width).astype(BF)
    second_ref[...] = out_ref[1].reshape(ranks, rows, width).astype(BF)


def share_kernel(got_ref, half_ref, sent_ref):
    ranks, rows, width = got_ref.shape
    part = ranks // 16
    total = got_ref[0:part].astype(F32)
    for i in range(1, 16):
        total = total + got_ref[i * part : (i + 1) * part].astype(F32)
    total = jnp.sum(total, axis=0, keepdims=True).astype(BF)
    sent_ref[...] = jnp.where(iota(got_ref.shape, 1) < 4, half_ref[...], total)


def field_kernel(
    first_ref, second_ref, order_ref, table_ref, grad_ref, out_ref, gain_ref, msg_ref, field_ref, share_ref, sems
):
    lat_dev, lons, width = grad_ref.shape
    ranks = first_ref.shape[0]
    half = lons // 2
    msg_ref[1] = second_ref[...].astype(F32).reshape(msg_ref.shape[1:])
    for g in range(2):
        for h in range(2):
            share_ref[g, h * ranks : (h + 1) * ranks, :] = msg_ref[
                1, pl.ds(4 + g * 2 + h, ranks, stride=8), :
            ]
    copies = [pltpu.make_async_copy(share_ref, gain_ref, sems.at[0])]
    copies[0].start()
    msg_ref[0] = first_ref[...].astype(F32).reshape(msg_ref.shape[1:])
    row = iota((half, ranks), 0)
    order = (row % ranks) * 2 + row // ranks
    chosen = [(order == order_ref[s : s + 1, :]).astype(BF) for s in range(2)]
    chosen = jnp.concatenate(chosen, axis=1)
    placed = []
    for r in range(2):
        parts = []
        for s in range(2):
            lanes = [msg_ref[s, pl.ds(r * 2 + k, ranks, stride=8), :].astype(BF) for k in range(2)]
            parts.append(jnp.concatenate(lanes, axis=1))
        placed.append(dot(chosen, jnp.concatenate(parts, axis=0)).astype(BF))
    even = jnp.concatenate([p[:ranks] for p in placed], axis=0)
    odd = jnp.concatenate([p[ranks:] for p in placed], axis=0)
    block = half // 4
    for i in range(4):
        rows = slice(i * block, (i + 1) * block)
        same = dot(table_ref[0, rows, :], even)
        turned = dot(table_ref[1, rows, :], odd)
        for h in range(2):
            span = slice(h * half + i * block, h * half + (i + 1) * block)
            for k in range(lat_dev):
                lanes = slice(k * width, (k + 1) * width)
                part = same[:, lanes] + turned[:, lanes] if h == 0 else same[:, lanes] - turned[:, lanes]
                field_ref[k, span, :] = (grad_ref[k, span, :] + part).astype(BF)
            copies.append(
                pltpu.make_async_copy(
                    field_ref.at[:, span, :], out_ref.at[:, span, :], sems.at[len(copies)]
                )
            )
            copies[-1].start()
    for copy in copies:
        copy.wait()


def exchange(message):
    return lax.all_to_all(message, RANKS, split_axis=0, concat_axis=0, tiled=True)


def on_device(
    next_grad,
    pre_act,
    legendre,
    order_slots,
    quad_weights,
    spectral_gain,
    saved_coeffs,
    obs_value,
    obs_lat_frac,
    obs_lon_frac,
    obs_corner,
    obs_channel,
    slot_counts,
):
    lat_dev, lons, width = next_grad.shape
    slot_dev, degrees, lats = legendre.shape
    orders = order_slots.shape[0]
    ranks = lax.axis_size("lat") * lax.axis_size("obs")
    shape = jax.ShapeDtypeStruct

    index = np.arange(orders)
    angle = ((index[:, None] * index[None, :]) % lons).astype(np.float32) * np.float32(
        2.0 * math.pi / lons
    )
    waves = np.stack([np.cos(angle), np.sin(angle)]).astype(jnp.bfloat16)
    table = jnp.asarray(waves)
    back = np.stack([waves[0].astype(np.float32), -waves[1].astype(np.float32)]) / lons
    back = [np.concatenate([back[0, :, p::2], back[1, :, p::2]], axis=1) for p in range(2)]
    back = jnp.asarray(np.stack(back).astype(jnp.bfloat16))

    core = lax.axis_index("chan").astype(jnp.int32).reshape(1)
    slot_args = (
        obs_value[0],
        obs_lat_frac[0],
        obs_lon_frac[0],
        obs_corner[0],
        obs_channel[0],
        slot_counts,
    )
    packed = call(
        pack_kernel,
        shape((ranks, 128), F32),
        scratch=buffers_for(slot_args),
        smem=1,
        far=range(1, 7),
        limit=60,
    )(core * width, *slot_args)

    ready_args = (legendre, quad_weights.reshape(1, lats))
    ready = (
        shape(legendre.shape, BF),
        shape((slot_dev, lats, degrees), BF),
        shape((lats, 128), F32),
    )

    def prepare(turn, before=()):
        return call(
            ready_kernel,
            ready,
            scratch=buffers_for(ready_args)[:-1]
            + buffers_for(ready)[:-1]
            + [pltpu.SemaphoreType.DMA((8,))],
            smem=1,
            far=range(1, 6),
            far_out=True,
            aliases={3 + i: i for i in range(len(before))},
            flops=4 * 2 * 512**3,
            limit=60,
        )(turn, *ready_args, *before)

    early_args = (order_slots.reshape(1, orders), table)
    early = call(
        early_kernel,
        shape(table.shape, BF),
        scratch=buffers_for(early_args)[:-1]
        + [pltpu.VMEM(table.shape, BF), pltpu.SemaphoreType.DMA((2,))],
        smem=1,
        far=range(1, 3),
        far_out=True,
        flops=2 * 2 * 512**3,
        limit=60,
    )(1 - core, *early_args)
    packed, prepared, early = lax.optimization_barrier((packed, prepare(1 - core), early))
    slots = exchange(packed)
    prepared = prepare(core, prepared)
    order_columns = order_slots.reshape(ranks, 2)
    slots, prepared, order_columns, order_rows = lax.optimization_barrier(
        (slots, prepared, order_columns, order_columns.T)
    )
    up_table, down_table, weight = prepared

    message = shape((ranks, 8, width), BF)
    rows = pltpu.VMEM((ranks * 8, width), F32)
    pairs = pltpu.VMEM((2, ranks * 8, width), F32)
    field = shape(next_grad.shape, F32)
    sent, out_grad = call(
        synth_kernel,
        (message, field),
        scratch=[
            pltpu.VMEM(field.shape, F32),
            pltpu.VMEM((lons // 4, 16 * ranks), BF),
            pltpu.VMEM((10 * width, 16 * ranks), BF),
            pltpu.VMEM(field.shape, F32),
            pltpu.VMEM((lons // 2, 2 * lat_dev * width), BF),
            rows,
        ],
        smem=1,
        flops=2 * 1024 * 4096 * 512,
        limit=32,
    )(core, slots, next_grad, pre_act, table, early, order_columns)
    by_order = exchange(sent)
    first, second = call(
        legendre_kernel, (message, message), scratch=[rows, pairs], flops=2 * 512**3 * 4
    )(by_order, up_table, down_table, weight, saved_coeffs, spectral_gain)
    first = exchange(first)
    second = exchange(call(share_kernel, message)(first, second))
    outs = (shape(next_grad.shape, BF), shape((2, degrees, width), F32))
    return call(
        field_kernel,
        outs,
        scratch=[pairs]
        + [pltpu.VMEM(o.shape, o.dtype) for o in outs]
        + [pltpu.SemaphoreType.DMA((9,))],
        far_out=True,
        flops=2 * 512**3 * 3,
    )(first, second, order_rows, back, out_grad)


def solution(mesh):
    ranks = P(RANKS, None, None)
    in_specs = (
        P(RANKS, None, "chan"),
        P(RANKS, None, "chan"),
        ranks,
        P(),
        P(),
        P(None, None, "chan"),
        P(RANKS, None, None, "chan"),
        ranks,
        ranks,
        ranks,
        ranks,
        ranks,
        P(RANKS, None),
    )
    out_specs = (P(RANKS, None, "chan"), P(None, None, "chan"))
    return jax.shard_map(
        on_device, mesh=mesh, in_specs=in_specs, out_specs=out_specs, check_vma=False
    )
```

```python
import math

import jax
import jax.numpy as jnp
import numpy as np
from jax import lax
from jax.experimental import pallas as pl
from jax.experimental.pallas import tpu as pltpu
from jax.sharding import PartitionSpec as P

BF = jnp.bfloat16
F32 = jnp.float32
NT = (((1,), (1,)), ((), ()))
RANKS = ("lat", "obs")


def dot(left, right):
    return jnp.dot(left, right, preferred_element_type=F32)


def dot_nt(left, right):
    return lax.dot_general(left, right, NT, preferred_element_type=F32)


def call(kernel, out_shape, scratch=(), smem=0, far=(), far_out=False, aliases=None, flops=0, limit=16):
    outs = out_shape if isinstance(out_shape, tuple) else (out_shape,)
    moved = sum(math.prod(o.shape) * o.dtype.itemsize for o in outs)

    def run(*args):
        specs = [
            pl.BlockSpec(
                memory_space=pltpu.SMEM if i < smem else pltpu.HBM if i in far else pltpu.VMEM
            )
            for i in range(len(args))
        ]
        total = moved + sum(math.prod(a.shape) * a.dtype.itemsize for a in args)
        return pl.pallas_call(
            kernel,
            out_shape=out_shape,
            in_specs=specs,
            out_specs=jax.tree.map(
                lambda _: pl.BlockSpec(memory_space=pltpu.HBM if far_out else pltpu.VMEM), out_shape
            ),
            scratch_shapes=list(scratch),
            input_output_aliases=aliases or {},
            compiler_params=pltpu.CompilerParams(vmem_limit_bytes=limit << 20),
            cost_estimate=pl.CostEstimate(flops=flops, bytes_accessed=total, transcendentals=0),
        )(*args)

    return run


def buffers_for(arrays):
    return [pltpu.VMEM(a.shape, a.dtype) for a in arrays] + [pltpu.SemaphoreType.DMA((len(arrays),))]


def start_copies(sources, targets, sems):
    copies = [
        pltpu.make_async_copy(source, target, sems.at[i])
        for i, (source, target) in enumerate(zip(sources, targets))
    ]
    for copy in copies:
        copy.start()
    return copies


def iota(shape, axis):
    return lax.broadcasted_iota(jnp.int32, shape, axis)


def pack_kernel(base_ref, *refs):
    sources, out_ref, buffers, sems = refs[:6], refs[6], refs[7:13], refs[13]
    for copy in start_copies(sources, buffers, sems):
        copy.wait()
    value, lat_frac, lon_frac, corner, chan, counts = [buffer[...] for buffer in buffers]
    capacity, tiles = value.shape
    alive = iota((capacity, tiles), 0) < counts
    fields = [
        jnp.where(alive, value.astype(F32), 0.0),
        lat_frac.astype(F32),
        lon_frac.astype(F32),
        corner.astype(F32),
        (chan - base_ref[0]).astype(F32),
        jnp.zeros((128 - 5 * capacity, tiles), F32),
    ]
    out_ref[...] = jnp.concatenate(fields, axis=0).T


def parted(count):
    place = iota((count, count), 0)
    return (place % (count // 2)) * 2 + place // (count // 2) == iota((count, count), 1)


def legendre_tables(chosen, sources, buffers, results, far, sems):
    legendre_ref, quad_ref = buffers
    up_ref, down_ref, weight_ref = results
    coming = [pltpu.make_async_copy(sources[0].at[s], legendre_ref.at[s], sems.at[s]) for s in range(2)]
    coming.append(pltpu.make_async_copy(sources[1], quad_ref, sems.at[2]))
    leaving = [pltpu.make_async_copy(weight_ref, far[2], sems.at[3])]
    for s in range(2):
        leaving.append(pltpu.make_async_copy(up_ref.at[s], far[0].at[s], sems.at[4 + 2 * s]))
        leaving.append(pltpu.make_async_copy(down_ref.at[s], far[1].at[s], sems.at[5 + 2 * s]))
    for copy in coming:
        copy.start()

    def work():
        pick = chosen.astype(BF)
        for s in range(2):
            coming[s].wait()
            up_ref[s] = dot_nt(legendre_ref[s], pick).astype(BF)
            leaving[1 + 2 * s].start()
            down_ref[s] = dot_nt(pick, legendre_ref[s]).astype(BF)
            leaving[2 + 2 * s].start()
        coming[2].wait()
        quad = jnp.sum(jnp.where(chosen, quad_ref[...], 0.0), axis=1, keepdims=True)
        weight_ref[...] = jnp.broadcast_to(quad, weight_ref.shape)
        leaving[0].start()

    return work, leaving


def ready_kernel(turn_ref, far_legendre, far_quad, _up, _down, _weight, *refs):
    far, buffers, results, sems = refs[:3], refs[3:5], refs[5:8], refs[8]

    @pl.when(turn_ref[0] == 1)
    def _():
        chosen = parted(buffers[0].shape[2])
        work, leaving = legendre_tables(chosen, (far_legendre, far_quad), buffers, results, far, sems)
        work()
        for copy in leaving:
            copy.wait()


def early_kernel(turn_ref, far_legendre, far_quad, far_order, far_table, *refs):
    far, far_early, buffers, results, sems = refs[:3], refs[3], refs[4:6], refs[6:9], refs[9]
    order_ref, table_ref, early_ref, more_sems = refs[10:]

    @pl.when(turn_ref[0] == 1)
    def _():
        chosen = parted(buffers[0].shape[2])
        work, leaving = legendre_tables(chosen, (far_legendre, far_quad), buffers, results, far, sems)
        coming = start_copies((far_order, far_table), (order_ref, table_ref), more_sems)
        work()
        coming[0].wait()
        orders = table_ref.shape[1]
        order = jnp.where(chosen, order_ref[...].astype(F32), 0.0)
        order = jnp.sum(order, axis=1, keepdims=True).astype(jnp.int32)
        scale = jnp.where(order == 0, 1.0, 2.0)
        placed = (iota((orders, orders), 1) == order).astype(BF)
        coming[1].wait()
        for r in range(2):
            early_ref[r] = (dot(placed, table_ref[r]) * (scale if r == 0 else -scale)).astype(BF)
            copy = pltpu.make_async_copy(early_ref.at[r], far_early.at[r], more_sems.at[2 + r])
            copy.start()
            leaving.append(copy)
        for copy in leaving:
            copy.wait()


def tall(row, count):
    block = jnp.broadcast_to(row, (16, row.shape[1])).astype(BF)
    return jnp.concatenate([block] * (count // 16), axis=0)


def synth_kernel(
    core_ref,
    slots_ref,
    next_ref,
    pre_ref,
    table_ref,
    early_ref,
    order_ref,
    sent_ref,
    grad_ref,
    slope_ref,
    rows_ref,
    cols_ref,
    field_ref,
    halves_ref,
    msg_ref,
):
    values = pre_ref[...].astype(F32)
    cdf = 0.5 * (1.0 + lax.erf(values * 0.7071067811865476))
    density = jnp.exp(-0.5 * values * values) * 0.3989422804014327
    slope_ref[...] = cdf + values * density
    lat_dev, lons, width = next_ref.shape
    ranks = slots_ref.shape[0]
    capacity = 16
    groups = lons // 4
    orders = table_ref.shape[1]
    fields = slots_ref[...].T
    value = fields[0:16]
    lat_step = fields[16:32]
    lon_step = fields[32:48]
    corner = fields[48:64].astype(jnp.int32)
    chan = fields[64:80]
    group = (corner // 4).astype(F32)
    place = corner % 4
    at_left = ((1.0 - lat_step) * (1.0 - lon_step), lat_step * (1.0 - lon_step))
    at_right = ((1.0 - lat_step) * lon_step, lat_step * lon_step)
    weights = [
        jnp.where(place == j, at_left[k], 0.0) + jnp.where(place == j - 1, at_right[k], 0.0)
        for j in range(5)
        for k in range(lat_dev)
    ]
    chan_ids = iota((width, ranks), 0).astype(F32).astype(BF)
    group_ids = iota((groups, ranks), 0).astype(F32).astype(BF)
    nothing = jnp.zeros((), BF)
    for p in range(capacity):
        span = slice(p * ranks, (p + 1) * ranks)
        rows_ref[:, span] = jnp.where(
            group_ids == tall(group[p : p + 1], groups), tall(value[p : p + 1], groups), nothing
        )
        hit = chan_ids == tall(chan[p : p + 1], width)
        for i, weight in enumerate(weights):
            cols_ref[i * width : (i + 1) * width, span] = jnp.where(
                hit, tall(weight[p : p + 1], width), nothing
            )
    pair = lat_dev * width
    found = [
        dot_nt(rows_ref[...], cols_ref[j * pair : (j + 1) * pair, :]) for j in range(5)
    ]
    found[0] = found[0] + pltpu.roll(found[4], 1, 0)
    for j in range(4):
        for k in range(lat_dev):
            field_ref[k, pl.ds(j, groups, stride=4), :] = found[j][:, k * width : (k + 1) * width]
    halves = []
    for h in range(2):
        at = h * (lons // 2)
        parts = []
        for k in range(lat_dev):
            total = next_ref[k, at : at + lons // 2, :].astype(F32) + field_ref[
                k, at : at + lons // 2, :
            ]
            grad_ref[k, at : at + lons // 2, :] = total
            parts.append((total * slope_ref[k, at : at + lons // 2, :]).astype(BF))
        halves.extend(parts)
    halves_ref[...] = jnp.concatenate(halves, axis=1)

    def store(total, r):
        for s in range(2):
            for k in range(lat_dev):
                msg_ref[pl.ds(s * 4 + r * 2 + k, ranks, stride=8), :] = total[
                    s * ranks : (s + 1) * ranks, k * width : (k + 1) * width
                ]

    @pl.when(core_ref[0] == 0)
    def _():
        order = jnp.concatenate([order_ref[:, s : s + 1] for s in range(2)], axis=0)
        sign = jnp.where(order % 2 == 0, 1.0, -1.0)
        for r in range(2):
            both = dot(early_ref[r], halves_ref[...])
            store(both[:, :pair] + sign * both[:, pair:], r)

    @pl.when(core_ref[0] == 1)
    def _():
        chosen = [
            (iota((ranks, orders), 1) == order_ref[:, s : s + 1]).astype(BF) for s in range(2)
        ]
        chosen = jnp.concatenate(chosen, axis=0)
        order_ids = iota((orders, 1), 0)
        sign = jnp.where(order_ids % 2 == 0, 1.0, -1.0)
        scale = jnp.where(order_ids == 0, 1.0, 2.0)
        totals = []
        for r in range(2):
            both = dot(table_ref[r], halves_ref[...])
            total = (both[:, :pair] + sign * both[:, pair:]) * (scale if r == 0 else -scale)
            totals.append(total.astype(BF))
        placed = dot(chosen, jnp.concatenate(totals, axis=1))
        for r in range(2):
            store(placed[:, r * pair : (r + 1) * pair], r)

    sent_ref[...] = msg_ref[...].reshape(ranks, 8, width).astype(BF)


def legendre_kernel(
    got_ref, up_ref, down_ref, weight_ref, saved_ref, gain_ref, first_ref, second_ref, msg_ref, out_ref
):
    ranks, rows, width = got_ref.shape
    msg_ref[...] = got_ref[...].astype(F32).reshape(ranks * rows, width)
    gain_real = gain_ref[0]
    gain_imag = gain_ref[1]
    terms = [None, None]
    for s in range(2):
        parts = []
        for r in range(2):
            lanes = [
                msg_ref[pl.ds(s * 4 + r * 2 + k, ranks, stride=8), :].astype(BF) for k in range(2)
            ]
            parts.append(jnp.concatenate(lanes, axis=0))
        found = dot(up_ref[s], jnp.concatenate(parts, axis=1))
        real = found[:, :width]
        imag = found[:, width:]
        saved_real = saved_ref[s, 0].astype(F32)
        saved_imag = saved_ref[s, 1].astype(F32)
        new = (real * saved_real + imag * saved_imag, imag * saved_real - real * saved_imag)
        terms = [n if t is None else t + n for t, n in zip(terms, new)]
        coeff = jnp.concatenate(
            [gain_real * real + gain_imag * imag, gain_real * imag - gain_imag * real], axis=1
        ).astype(BF)
        lat_grad = dot(down_ref[s], coeff)
        for r in range(2):
            weighted = lat_grad[:, r * width : (r + 1) * width] * weight_ref[...]
            for k in range(2):
                out_ref[s, pl.ds(r * 2 + k, ranks, stride=8), :] = weighted[
                    k * ranks : (k + 1) * ranks
                ]
    for g in range(2):
        for h in range(2):
            part = terms[g][h * ranks : (h + 1) * ranks]
            for s in range(2):
                out_ref[s, pl.ds(4 + g * 2 + h, ranks, stride=8), :] = part
    first_ref[...] = out_ref[0].reshape(ranks, rows, width).astype(BF)
    second_ref[...] = out_ref[1].reshape(ranks, rows, width).astype(BF)


def share_kernel(got_ref, half_ref, sent_ref):
    ranks, rows, width = got_ref.shape
    part = ranks // 16
    total = got_ref[0:part].astype(F32)
    for i in range(1, 16):
        total = total + got_ref[i * part : (i + 1) * part].astype(F32)
    total = jnp.sum(total, axis=0, keepdims=True).astype(BF)
    sent_ref[...] = jnp.where(iota(got_ref.shape, 1) < 4, half_ref[...], total)


def field_kernel(
    first_ref, second_ref, order_ref, table_ref, grad_ref, out_ref, gain_ref, msg_ref, field_ref, share_ref, sems
):
    lat_dev, lons, width = grad_ref.shape
    ranks = first_ref.shape[0]
    half = lons // 2
    msg_ref[1] = second_ref[...].astype(F32).reshape(msg_ref.shape[1:])
    for g in range(2):
        for h in range(2):
            share_ref[g, h * ranks : (h + 1) * ranks, :] = msg_ref[
                1, pl.ds(4 + g * 2 + h, ranks, stride=8), :
            ]
    copies = [pltpu.make_async_copy(share_ref, gain_ref, sems.at[0])]
    copies[0].start()
    msg_ref[0] = first_ref[...].astype(F32).reshape(msg_ref.shape[1:])
    row = iota((half, ranks), 0)
    order = (row % ranks) * 2 + row // ranks
    chosen = [(order == order_ref[s : s + 1, :]).astype(BF) for s in range(2)]
    chosen = jnp.concatenate(chosen, axis=1)
    placed = []
    for r in range(2):
        parts = []
        for s in range(2):
            lanes = [msg_ref[s, pl.ds(r * 2 + k, ranks, stride=8), :].astype(BF) for k in range(2)]
            parts.append(jnp.concatenate(lanes, axis=1))
        placed.append(dot(chosen, jnp.concatenate(parts, axis=0)).astype(BF))
    even = jnp.concatenate([p[:ranks] for p in placed], axis=0)
    odd = jnp.concatenate([p[ranks:] for p in placed], axis=0)
    block = half // 4
    for i in range(4):
        rows = slice(i * block, (i + 1) * block)
        same = dot(table_ref[0, rows, :], even)
        turned = dot(table_ref[1, rows, :], odd)
        for h in range(2):
            span = slice(h * half + i * block, h * half + (i + 1) * block)
            for k in range(lat_dev):
                lanes = slice(k * width, (k + 1) * width)
                part = same[:, lanes] + turned[:, lanes] if h == 0 else same[:, lanes] - turned[:, lanes]
                field_ref[k, span, :] = (grad_ref[k, span, :] + part).astype(BF)
            copies.append(
                pltpu.make_async_copy(
                    field_ref.at[:, span, :], out_ref.at[:, span, :], sems.at[len(copies)]
                )
            )
            copies[-1].start()
    for copy in copies:
        copy.wait()


def exchange(message):
    return lax.all_to_all(message, RANKS, split_axis=0, concat_axis=0, tiled=True)


def on_device(
    next_grad,
    pre_act,
    legendre,
    order_slots,
    quad_weights,
    spectral_gain,
    saved_coeffs,
    obs_value,
    obs_lat_frac,
    obs_lon_frac,
    obs_corner,
    obs_channel,
    slot_counts,
):
    lat_dev, lons, width = next_grad.shape
    slot_dev, degrees, lats = legendre.shape
    orders = order_slots.shape[0]
    ranks = lax.axis_size("lat") * lax.axis_size("obs")
    shape = jax.ShapeDtypeStruct

    index = np.arange(orders)
    angle = ((index[:, None] * index[None, :]) % lons).astype(np.float32) * np.float32(
        2.0 * math.pi / lons
    )
    waves = np.stack([np.cos(angle), np.sin(angle)]).astype(jnp.bfloat16)
    table = jnp.asarray(waves)
    back = np.stack([waves[0].astype(np.float32), -waves[1].astype(np.float32)]) / lons
    back = [np.concatenate([back[0, :, p::2], back[1, :, p::2]], axis=1) for p in range(2)]
    back = jnp.asarray(np.stack(back).astype(jnp.bfloat16))

    core = lax.axis_index("chan").astype(jnp.int32).reshape(1)
    slot_args = (
        obs_value[0],
        obs_lat_frac[0],
        obs_lon_frac[0],
        obs_corner[0],
        obs_channel[0],
        slot_counts,
    )
    packed = call(
        pack_kernel,
        shape((ranks, 128), F32),
        scratch=buffers_for(slot_args),
        smem=1,
        far=range(1, 7),
        limit=60,
    )(core * width, *slot_args)

    ready_args = (legendre, quad_weights.reshape(1, lats))
    ready = (
        shape(legendre.shape, BF),
        shape((slot_dev, lats, degrees), BF),
        shape((lats, 128), F32),
    )
    ready_scratch = (
        buffers_for(ready_args)[:-1] + buffers_for(ready)[:-1] + [pltpu.SemaphoreType.DMA((8,))]
    )
    early_args = (order_slots.reshape(1, orders), table)

    *prepared, early = call(
        early_kernel,
        (*ready, shape(table.shape, BF)),
        scratch=ready_scratch
        + buffers_for(early_args)[:-1]
        + [pltpu.VMEM(table.shape, BF), pltpu.SemaphoreType.DMA((4,))],
        smem=1,
        far=range(1, 5),
        far_out=True,
        flops=6 * 2 * 512**3,
        limit=60,
    )(1 - core, *ready_args, *early_args)
    packed, prepared, early = lax.optimization_barrier((packed, prepared, early))
    slots = exchange(packed)
    prepared = call(
        ready_kernel,
        ready,
        scratch=ready_scratch,
        smem=1,
        far=range(1, 6),
        far_out=True,
        aliases={3: 0, 4: 1, 5: 2},
        flops=4 * 2 * 512**3,
        limit=60,
    )(core, *ready_args, *prepared)
    order_columns = order_slots.reshape(ranks, 2)
    slots, prepared, order_columns, order_rows = lax.optimization_barrier(
        (slots, prepared, order_columns, order_columns.T)
    )
    up_table, down_table, weight = prepared

    message = shape((ranks, 8, width), BF)
    rows = pltpu.VMEM((ranks * 8, width), F32)
    pairs = pltpu.VMEM((2, ranks * 8, width), F32)
    field = shape(next_grad.shape, F32)
    sent, out_grad = call(
        synth_kernel,
        (message, field),
        scratch=[
            pltpu.VMEM(field.shape, F32),
            pltpu.VMEM((lons // 4, 16 * ranks), BF),
            pltpu.VMEM((10 * width, 16 * ranks), BF),
            pltpu.VMEM(field.shape, F32),
            pltpu.VMEM((lons // 2, 2 * lat_dev * width), BF),
            rows,
        ],
        smem=1,
        flops=2 * 1024 * 4096 * 512,
        limit=32,
    )(core, slots, next_grad, pre_act, table, early, order_columns)
    by_order = exchange(sent)
    first, second = call(
        legendre_kernel, (message, message), scratch=[rows, pairs], flops=2 * 512**3 * 4
    )(by_order, up_table, down_table, weight, saved_coeffs, spectral_gain)
    first = exchange(first)
    second = exchange(call(share_kernel, message)(first, second))
    outs = (shape(next_grad.shape, BF), shape((2, degrees, width), F32))
    return call(
        field_kernel,
        outs,
        scratch=[pairs]
        + [pltpu.VMEM(o.shape, o.dtype) for o in outs]
        + [pltpu.SemaphoreType.DMA((9,))],
        far_out=True,
        flops=2 * 512**3 * 3,
    )(first, second, order_rows, back, out_grad)


def solution(mesh):
    ranks = P(RANKS, None, None)
    in_specs = (
        P(RANKS, None, "chan"),
        P(RANKS, None, "chan"),
        ranks,
        P(),
        P(),
        P(None, None, "chan"),
        P(RANKS, None, None, "chan"),
        ranks,
        ranks,
        ranks,
        ranks,
        ranks,
        P(RANKS, None),
    )
    out_specs = (P(RANKS, None, "chan"), P(None, None, "chan"))
    return jax.shard_map(
        on_device, mesh=mesh, in_specs=in_specs, out_specs=out_specs, check_vma=False
    )
```

```python
import math

import jax
import jax.numpy as jnp
import numpy as np
from jax import lax
from jax.experimental import pallas as pl
from jax.experimental.pallas import tpu as pltpu
from jax.sharding import PartitionSpec as P

BF = jnp.bfloat16
F32 = jnp.float32
NT = (((1,), (1,)), ((), ()))
RANKS = ("lat", "obs")


def dot(left, right):
    return jnp.dot(left, right, preferred_element_type=F32)


def dot_nt(left, right):
    return lax.dot_general(left, right, NT, preferred_element_type=F32)


def call(kernel, out_shape, scratch=(), smem=0, far=(), far_out=False, aliases=None, flops=0, limit=16):
    outs = out_shape if isinstance(out_shape, tuple) else (out_shape,)
    moved = sum(math.prod(o.shape) * o.dtype.itemsize for o in outs)

    def run(*args):
        specs = [
            pl.BlockSpec(
                memory_space=pltpu.SMEM if i < smem else pltpu.HBM if i in far else pltpu.VMEM
            )
            for i in range(len(args))
        ]
        total = moved + sum(math.prod(a.shape) * a.dtype.itemsize for a in args)
        return pl.pallas_call(
            kernel,
            out_shape=out_shape,
            in_specs=specs,
            out_specs=jax.tree.map(
                lambda _: pl.BlockSpec(memory_space=pltpu.HBM if far_out else pltpu.VMEM), out_shape
            ),
            scratch_shapes=list(scratch),
            input_output_aliases=aliases or {},
            compiler_params=pltpu.CompilerParams(vmem_limit_bytes=limit << 20),
            cost_estimate=pl.CostEstimate(flops=flops, bytes_accessed=total, transcendentals=0),
        )(*args)

    return run


def buffers_for(arrays):
    return [pltpu.VMEM(a.shape, a.dtype) for a in arrays] + [pltpu.SemaphoreType.DMA((len(arrays),))]


def start_copies(sources, targets, sems):
    copies = [
        pltpu.make_async_copy(source, target, sems.at[i])
        for i, (source, target) in enumerate(zip(sources, targets))
    ]
    for copy in copies:
        copy.start()
    return copies


def iota(shape, axis):
    return lax.broadcasted_iota(jnp.int32, shape, axis)


def pack_kernel(base_ref, *refs):
    sources, out_ref, buffers, sems = refs[:6], refs[6], refs[7:13], refs[13]
    for copy in start_copies(sources, buffers, sems):
        copy.wait()
    value, lat_frac, lon_frac, corner, chan, counts = [buffer[...] for buffer in buffers]
    capacity, tiles = value.shape
    alive = iota((capacity, tiles), 0) < counts
    fields = [
        jnp.where(alive, value.astype(F32), 0.0),
        lat_frac.astype(F32),
        lon_frac.astype(F32),
        corner.astype(F32),
        (chan - base_ref[0]).astype(F32),
        jnp.zeros((128 - 5 * capacity, tiles), F32),
    ]
    out_ref[...] = jnp.concatenate(fields, axis=0).T


def parted(count):
    place = iota((count, count), 0)
    return (place % (count // 2)) * 2 + place // (count // 2) == iota((count, count), 1)


def legendre_tables(chosen, sources, buffers, results, far, sems):
    legendre_ref, quad_ref = buffers
    up_ref, down_ref, weight_ref = results
    coming = [pltpu.make_async_copy(sources[0].at[s], legendre_ref.at[s], sems.at[s]) for s in range(2)]
    coming.append(pltpu.make_async_copy(sources[1], quad_ref, sems.at[2]))
    leaving = [pltpu.make_async_copy(weight_ref, far[2], sems.at[3])]
    for s in range(2):
        leaving.append(pltpu.make_async_copy(up_ref.at[s], far[0].at[s], sems.at[4 + 2 * s]))
        leaving.append(pltpu.make_async_copy(down_ref.at[s], far[1].at[s], sems.at[5 + 2 * s]))
    for copy in coming:
        copy.start()

    def work():
        pick = chosen.astype(BF)
        for s in range(2):
            coming[s].wait()
            up_ref[s] = dot_nt(legendre_ref[s], pick).astype(BF)
            leaving[1 + 2 * s].start()
            down_ref[s] = dot_nt(pick, legendre_ref[s]).astype(BF)
            leaving[2 + 2 * s].start()
        coming[2].wait()
        quad = jnp.sum(jnp.where(chosen, quad_ref[...], 0.0), axis=1, keepdims=True)
        weight_ref[...] = jnp.broadcast_to(quad, weight_ref.shape)
        leaving[0].start()

    return work, leaving


def ready_kernel(turn_ref, far_legendre, far_quad, _up, _down, _weight, *refs):
    far, buffers, results, sems = refs[:3], refs[3:5], refs[5:8], refs[8]

    @pl.when(turn_ref[0] == 1)
    def _():
        chosen = parted(buffers[0].shape[2])
        work, leaving = legendre_tables(chosen, (far_legendre, far_quad), buffers, results, far, sems)
        work()
        for copy in leaving:
            copy.wait()


def early_kernel(turn_ref, far_legendre, far_quad, far_order, far_table, *refs):
    far, far_early, buffers, results, sems = refs[:3], refs[3], refs[4:6], refs[6:9], refs[9]
    order_ref, table_ref, early_ref, more_sems = refs[10:]

    @pl.when(turn_ref[0] == 1)
    def _():
        chosen = parted(buffers[0].shape[2])
        work, leaving = legendre_tables(chosen, (far_legendre, far_quad), buffers, results, far, sems)
        coming = start_copies((far_order, far_table), (order_ref, table_ref), more_sems)
        work()
        coming[0].wait()
        orders = table_ref.shape[1]
        order = jnp.where(chosen, order_ref[...].astype(F32), 0.0)
        order = jnp.sum(order, axis=1, keepdims=True).astype(jnp.int32)
        scale = jnp.where(order == 0, 1.0, 2.0)
        placed = (iota((orders, orders), 1) == order).astype(BF)
        coming[1].wait()
        for r in range(2):
            early_ref[r] = (dot(placed, table_ref[r]) * (scale if r == 0 else -scale)).astype(BF)
            copy = pltpu.make_async_copy(early_ref.at[r], far_early.at[r], more_sems.at[2 + r])
            copy.start()
            leaving.append(copy)
        for copy in leaving:
            copy.wait()


def tall(row, count):
    block = jnp.broadcast_to(row, (16, row.shape[1])).astype(BF)
    return jnp.concatenate([block] * (count // 16), axis=0)


def synth_kernel(
    core_ref,
    slots_ref,
    next_ref,
    pre_ref,
    table_ref,
    early_ref,
    order_ref,
    sent_ref,
    grad_ref,
    slope_ref,
    rows_ref,
    cols_ref,
    field_ref,
    halves_ref,
    total_ref,
    msg_ref,
):
    values = pre_ref[...].astype(F32)
    cdf = 0.5 * (1.0 + lax.erf(values * 0.7071067811865476))
    density = jnp.exp(-0.5 * values * values) * 0.3989422804014327
    slope_ref[...] = cdf + values * density
    lat_dev, lons, width = next_ref.shape
    ranks = slots_ref.shape[0]
    capacity = 16
    groups = lons // 4
    orders = table_ref.shape[1]
    fields = slots_ref[...].T
    value = fields[0:16]
    lat_step = fields[16:32]
    lon_step = fields[32:48]
    corner = fields[48:64].astype(jnp.int32)
    chan = fields[64:80]
    group = (corner // 4).astype(F32)
    place = corner % 4
    at_left = ((1.0 - lat_step) * (1.0 - lon_step), lat_step * (1.0 - lon_step))
    at_right = ((1.0 - lat_step) * lon_step, lat_step * lon_step)
    weights = [
        jnp.where(place == j, at_left[k], 0.0) + jnp.where(place == j - 1, at_right[k], 0.0)
        for j in range(5)
        for k in range(lat_dev)
    ]
    chan_ids = iota((width, ranks), 0).astype(F32).astype(BF)
    group_ids = iota((groups, ranks), 0).astype(F32).astype(BF)
    nothing = jnp.zeros((), BF)
    for p in range(capacity):
        span = slice(p * ranks, (p + 1) * ranks)
        rows_ref[:, span] = jnp.where(
            group_ids == tall(group[p : p + 1], groups), tall(value[p : p + 1], groups), nothing
        )
        hit = chan_ids == tall(chan[p : p + 1], width)
        for i, weight in enumerate(weights):
            cols_ref[i * width : (i + 1) * width, span] = jnp.where(
                hit, tall(weight[p : p + 1], width), nothing
            )
    pair = lat_dev * width

    def found(j):
        return dot_nt(rows_ref[...], cols_ref[j * pair : (j + 1) * pair, :])

    for j in range(4):
        part = found(j)
        if j == 0:
            part = part + pltpu.roll(found(4), 1, 0)
        for k in range(lat_dev):
            field_ref[k, pl.ds(j, groups, stride=4), :] = part[:, k * width : (k + 1) * width]
    block = 128
    for k in range(lat_dev):
        for h in range(2):
            lanes = slice(h * pair + k * width, h * pair + (k + 1) * width)
            for i in range(lons // 2 // block):
                span = slice(h * lons // 2 + i * block, h * lons // 2 + (i + 1) * block)
                total = next_ref[k, span, :].astype(F32) + field_ref[k, span, :]
                grad_ref[k, span, :] = total
                halves_ref[i * block : (i + 1) * block, lanes] = (
                    total * slope_ref[k, span, :]
                ).astype(BF)

    def store(total, r):
        for s in range(2):
            for k in range(lat_dev):
                msg_ref[pl.ds(s * 4 + r * 2 + k, ranks, stride=8), :] = total[
                    s * ranks : (s + 1) * ranks, k * width : (k + 1) * width
                ]

    @pl.when(core_ref[0] == 0)
    def _():
        order = jnp.concatenate([order_ref[:, s : s + 1] for s in range(2)], axis=0)
        sign = jnp.where(order % 2 == 0, 1.0, -1.0)
        for r in range(2):
            both = dot(early_ref[r], halves_ref[...])
            store(both[:, :pair] + sign * both[:, pair:], r)

    @pl.when(core_ref[0] == 1)
    def _():
        chosen = [
            (iota((ranks, orders), 1) == order_ref[:, s : s + 1]).astype(BF) for s in range(2)
        ]
        chosen = jnp.concatenate(chosen, axis=0)
        order_ids = iota((orders, 1), 0)
        sign = jnp.where(order_ids % 2 == 0, 1.0, -1.0)
        scale = jnp.where(order_ids == 0, 1.0, 2.0)
        for r in range(2):
            both = dot(table_ref[r], halves_ref[...])
            total = (both[:, :pair] + sign * both[:, pair:]) * (scale if r == 0 else -scale)
            total_ref[:, r * pair : (r + 1) * pair] = total.astype(BF)
        for r in range(2):
            store(dot(chosen, total_ref[:, r * pair : (r + 1) * pair]), r)

    sent_ref[...] = msg_ref[...].reshape(ranks, 8, width).astype(BF)


def legendre_kernel(
    got_ref, up_ref, down_ref, weight_ref, saved_ref, gain_ref, first_ref, second_ref, msg_ref, out_ref, field_ref, coeff_ref
):
    ranks, rows, width = got_ref.shape
    msg_ref[...] = got_ref[...].astype(F32).reshape(ranks * rows, width)
    gain_real = gain_ref[0]
    gain_imag = gain_ref[1]
    terms = [None, None]
    for s in range(2):
        for r in range(2):
            for k in range(2):
                field_ref[s, k * ranks : (k + 1) * ranks, r * width : (r + 1) * width] = msg_ref[
                    pl.ds(s * 4 + r * 2 + k, ranks, stride=8), :
                ].astype(BF)
    for s in range(2):
        found = dot(up_ref[s], field_ref[s])
        real = found[:, :width]
        imag = found[:, width:]
        saved_real = saved_ref[s, 0].astype(F32)
        saved_imag = saved_ref[s, 1].astype(F32)
        coeff_ref[s, :, :width] = (gain_real * real + gain_imag * imag).astype(BF)
        coeff_ref[s, :, width:] = (gain_real * imag - gain_imag * real).astype(BF)
        new = (real * saved_real + imag * saved_imag, imag * saved_real - real * saved_imag)
        terms = [n if t is None else t + n for t, n in zip(terms, new)]
    for s in range(2):
        lat_grad = dot(down_ref[s], coeff_ref[s])
        for r in range(2):
            weighted = lat_grad[:, r * width : (r + 1) * width] * weight_ref[...]
            for k in range(2):
                out_ref[s, pl.ds(r * 2 + k, ranks, stride=8), :] = weighted[
                    k * ranks : (k + 1) * ranks
                ]
    for g in range(2):
        for h in range(2):
            part = terms[g][h * ranks : (h + 1) * ranks]
            for s in range(2):
                out_ref[s, pl.ds(4 + g * 2 + h, ranks, stride=8), :] = part
    first_ref[...] = out_ref[0].reshape(ranks, rows, width).astype(BF)
    second_ref[...] = out_ref[1].reshape(ranks, rows, width).astype(BF)


def share_kernel(got_ref, half_ref, sent_ref):
    ranks, rows, width = got_ref.shape
    part = ranks // 16
    total = got_ref[0:part].astype(F32)
    for i in range(1, 16):
        total = total + got_ref[i * part : (i + 1) * part].astype(F32)
    total = jnp.sum(total, axis=0, keepdims=True).astype(BF)
    sent_ref[...] = jnp.where(iota(got_ref.shape, 1) < 4, half_ref[...], total)


def field_kernel(
    first_ref, second_ref, order_ref, table_ref, grad_ref, out_ref, gain_ref, msg_ref, field_ref, share_ref, sems
):
    lat_dev, lons, width = grad_ref.shape
    ranks = first_ref.shape[0]
    half = lons // 2
    msg_ref[1] = second_ref[...].astype(F32).reshape(msg_ref.shape[1:])
    for g in range(2):
        for h in range(2):
            share_ref[g, h * ranks : (h + 1) * ranks, :] = msg_ref[
                1, pl.ds(4 + g * 2 + h, ranks, stride=8), :
            ]
    copies = [pltpu.make_async_copy(share_ref, gain_ref, sems.at[0])]
    copies[0].start()
    msg_ref[0] = first_ref[...].astype(F32).reshape(msg_ref.shape[1:])
    row = iota((half, ranks), 0)
    order = (row % ranks) * 2 + row // ranks
    chosen = [(order == order_ref[s : s + 1, :]).astype(BF) for s in range(2)]
    chosen = jnp.concatenate(chosen, axis=1)
    placed = []
    for r in range(2):
        parts = []
        for s in range(2):
            lanes = [msg_ref[s, pl.ds(r * 2 + k, ranks, stride=8), :].astype(BF) for k in range(2)]
            parts.append(jnp.concatenate(lanes, axis=1))
        placed.append(dot(chosen, jnp.concatenate(parts, axis=0)).astype(BF))
    even = jnp.concatenate([p[:ranks] for p in placed], axis=0)
    odd = jnp.concatenate([p[ranks:] for p in placed], axis=0)
    block = half // 4
    for i in range(4):
        rows = slice(i * block, (i + 1) * block)
        same = dot(table_ref[0, rows, :], even)
        turned = dot(table_ref[1, rows, :], odd)
        for h in range(2):
            span = slice(h * half + i * block, h * half + (i + 1) * block)
            for k in range(lat_dev):
                lanes = slice(k * width, (k + 1) * width)
                part = same[:, lanes] + turned[:, lanes] if h == 0 else same[:, lanes] - turned[:, lanes]
                field_ref[k, span, :] = (grad_ref[k, span, :] + part).astype(BF)
            copies.append(
                pltpu.make_async_copy(
                    field_ref.at[:, span, :], out_ref.at[:, span, :], sems.at[len(copies)]
                )
            )
            copies[-1].start()
    for copy in copies:
        copy.wait()


def exchange(message):
    return lax.all_to_all(message, RANKS, split_axis=0, concat_axis=0, tiled=True)


def on_device(
    next_grad,
    pre_act,
    legendre,
    order_slots,
    quad_weights,
    spectral_gain,
    saved_coeffs,
    obs_value,
    obs_lat_frac,
    obs_lon_frac,
    obs_corner,
    obs_channel,
    slot_counts,
):
    lat_dev, lons, width = next_grad.shape
    slot_dev, degrees, lats = legendre.shape
    orders = order_slots.shape[0]
    ranks = lax.axis_size("lat") * lax.axis_size("obs")
    shape = jax.ShapeDtypeStruct

    index = np.arange(orders)
    angle = ((index[:, None] * index[None, :]) % lons).astype(np.float32) * np.float32(
        2.0 * math.pi / lons
    )
    waves = np.stack([np.cos(angle), np.sin(angle)]).astype(jnp.bfloat16)
    table = jnp.asarray(waves)
    back = np.stack([waves[0].astype(np.float32), -waves[1].astype(np.float32)]) / lons
    back = [np.concatenate([back[0, :, p::2], back[1, :, p::2]], axis=1) for p in range(2)]
    back = jnp.asarray(np.stack(back).astype(jnp.bfloat16))

    core = lax.axis_index("chan").astype(jnp.int32).reshape(1)
    slot_args = (
        obs_value[0],
        obs_lat_frac[0],
        obs_lon_frac[0],
        obs_corner[0],
        obs_channel[0],
        slot_counts,
    )
    packed = call(
        pack_kernel,
        shape((ranks, 128), F32),
        scratch=buffers_for(slot_args),
        smem=1,
        far=range(1, 7),
        limit=60,
    )(core * width, *slot_args)

    ready_args = (legendre, quad_weights.reshape(1, lats))
    ready = (
        shape(legendre.shape, BF),
        shape((slot_dev, lats, degrees), BF),
        shape((lats, 128), F32),
    )
    ready_scratch = (
        buffers_for(ready_args)[:-1] + buffers_for(ready)[:-1] + [pltpu.SemaphoreType.DMA((8,))]
    )
    early_args = (order_slots.reshape(1, orders), table)

    *prepared, early = call(
        early_kernel,
        (*ready, shape(table.shape, BF)),
        scratch=ready_scratch
        + buffers_for(early_args)[:-1]
        + [pltpu.VMEM(table.shape, BF), pltpu.SemaphoreType.DMA((4,))],
        smem=1,
        far=range(1, 5),
        far_out=True,
        flops=6 * 2 * 512**3,
        limit=60,
    )(1 - core, *ready_args, *early_args)
    packed, prepared, early = lax.optimization_barrier((packed, prepared, early))
    slots = exchange(packed)
    prepared = call(
        ready_kernel,
        ready,
        scratch=ready_scratch,
        smem=1,
        far=range(1, 6),
        far_out=True,
        aliases={3: 0, 4: 1, 5: 2},
        flops=4 * 2 * 512**3,
        limit=60,
    )(core, *ready_args, *prepared)
    order_columns = order_slots.reshape(ranks, 2)
    slots, prepared, order_columns, order_rows = lax.optimization_barrier(
        (slots, prepared, order_columns, order_columns.T)
    )
    up_table, down_table, weight = prepared

    message = shape((ranks, 8, width), BF)
    rows = pltpu.VMEM((ranks * 8, width), F32)
    pairs = pltpu.VMEM((2, ranks * 8, width), F32)
    field = shape(next_grad.shape, F32)
    sent, out_grad = call(
        synth_kernel,
        (message, field),
        scratch=[
            pltpu.VMEM(field.shape, F32),
            pltpu.VMEM((lons // 4, 16 * ranks), BF),
            pltpu.VMEM((10 * width, 16 * ranks), BF),
            pltpu.VMEM(field.shape, F32),
            pltpu.VMEM((lons // 2, 2 * lat_dev * width), BF),
            pltpu.VMEM((orders, 2 * lat_dev * width), BF),
            rows,
        ],
        smem=1,
        flops=2 * 1024 * 4096 * 512,
        limit=32,
    )(core, slots, next_grad, pre_act, table, early, order_columns)
    by_order = exchange(sent)
    first, second = call(
        legendre_kernel,
        (message, message),
        scratch=[rows, pairs]
        + [pltpu.VMEM((slot_dev, n, 2 * width), BF) for n in (lats, degrees)],
        flops=2 * 512**3 * 4
    )(by_order, up_table, down_table, weight, saved_coeffs, spectral_gain)
    first = exchange(first)
    second = exchange(call(share_kernel, message)(first, second))
    outs = (shape(next_grad.shape, BF), shape((2, degrees, width), F32))
    return call(
        field_kernel,
        outs,
        scratch=[pairs]
        + [pltpu.VMEM(o.shape, o.dtype) for o in outs]
        + [pltpu.SemaphoreType.DMA((9,))],
        far_out=True,
        flops=2 * 512**3 * 3,
    )(first, second, order_rows, back, out_grad)


def solution(mesh):
    ranks = P(RANKS, None, None)
    in_specs = (
        P(RANKS, None, "chan"),
        P(RANKS, None, "chan"),
        ranks,
        P(),
        P(),
        P(None, None, "chan"),
        P(RANKS, None, None, "chan"),
        ranks,
        ranks,
        ranks,
        ranks,
        ranks,
        P(RANKS, None),
    )
    out_specs = (P(RANKS, None, "chan"), P(None, None, "chan"))
    return jax.shard_map(
        on_device, mesh=mesh, in_specs=in_specs, out_specs=out_specs, check_vma=False
    )
```

```python
import math

import jax
import jax.numpy as jnp
import numpy as np
from jax import lax
from jax.experimental import pallas as pl
from jax.experimental.pallas import tpu as pltpu
from jax.sharding import PartitionSpec as P

BF = jnp.bfloat16
F32 = jnp.float32
NT = (((1,), (1,)), ((), ()))
RANKS = ("lat", "obs")


def dot(left, right):
    return jnp.dot(left, right, preferred_element_type=F32)


def dot_nt(left, right):
    return lax.dot_general(left, right, NT, preferred_element_type=F32)


def call(kernel, out_shape, scratch=(), smem=0, far=(), far_out=False, aliases=None, flops=0, limit=16):
    outs = out_shape if isinstance(out_shape, tuple) else (out_shape,)
    moved = sum(math.prod(o.shape) * o.dtype.itemsize for o in outs)

    def run(*args):
        specs = [
            pl.BlockSpec(
                memory_space=pltpu.SMEM if i < smem else pltpu.HBM if i in far else pltpu.VMEM
            )
            for i in range(len(args))
        ]
        total = moved + sum(math.prod(a.shape) * a.dtype.itemsize for a in args)
        return pl.pallas_call(
            kernel,
            out_shape=out_shape,
            in_specs=specs,
            out_specs=jax.tree.map(
                lambda _: pl.BlockSpec(memory_space=pltpu.HBM if far_out else pltpu.VMEM), out_shape
            ),
            scratch_shapes=list(scratch),
            input_output_aliases=aliases or {},
            compiler_params=pltpu.CompilerParams(vmem_limit_bytes=limit << 20),
            cost_estimate=pl.CostEstimate(flops=flops, bytes_accessed=total, transcendentals=0),
        )(*args)

    return run


def buffers_for(arrays):
    return [pltpu.VMEM(a.shape, a.dtype) for a in arrays] + [pltpu.SemaphoreType.DMA((len(arrays),))]


def start_copies(sources, targets, sems):
    copies = [
        pltpu.make_async_copy(source, target, sems.at[i])
        for i, (source, target) in enumerate(zip(sources, targets))
    ]
    for copy in copies:
        copy.start()
    return copies


def iota(shape, axis):
    return lax.broadcasted_iota(jnp.int32, shape, axis)


def pack_kernel(base_ref, *refs):
    sources, out_ref, buffers, sems = refs[:6], refs[6], refs[7:13], refs[13]
    for copy in start_copies(sources, buffers, sems):
        copy.wait()
    value, lat_frac, lon_frac, corner, chan, counts = [buffer[...] for buffer in buffers]
    capacity, tiles = value.shape
    alive = iota((capacity, tiles), 0) < counts
    fields = [
        jnp.where(alive, value.astype(F32), 0.0),
        lat_frac.astype(F32),
        lon_frac.astype(F32),
        corner.astype(F32),
        (chan - base_ref[0]).astype(F32),
        jnp.zeros((128 - 5 * capacity, tiles), F32),
    ]
    out_ref[...] = jnp.concatenate(fields, axis=0).T


def parted(count):
    place = iota((count, count), 0)
    return (place % (count // 2)) * 2 + place // (count // 2) == iota((count, count), 1)


def legendre_tables(chosen, sources, buffers, results, far, sems):
    legendre_ref, quad_ref = buffers
    up_ref, down_ref, weight_ref = results
    coming = [pltpu.make_async_copy(sources[0].at[s], legendre_ref.at[s], sems.at[s]) for s in range(2)]
    coming.append(pltpu.make_async_copy(sources[1], quad_ref, sems.at[2]))
    leaving = [pltpu.make_async_copy(weight_ref, far[2], sems.at[3])]
    for s in range(2):
        leaving.append(pltpu.make_async_copy(up_ref.at[s], far[0].at[s], sems.at[4 + s]))
        for h in range(2):
            rows = slice(h * 256, (h + 1) * 256)
            leaving.append(
                pltpu.make_async_copy(
                    down_ref.at[s, rows], far[1].at[s, rows], sems.at[6 + 2 * s + h]
                )
            )
    for copy in coming[2:] + coming[:2]:
        copy.start()

    def work():
        coming[2].wait()
        quad = jnp.sum(jnp.where(chosen, quad_ref[...], 0.0), axis=1, keepdims=True)
        weight_ref[...] = jnp.broadcast_to(quad, weight_ref.shape)
        leaving[0].start()
        pick = chosen.astype(BF)
        for s in range(2):
            coming[s].wait()
            up_ref[s] = dot_nt(legendre_ref[s], pick).astype(BF)
            leaving[1 + 3 * s].start()
            for h in range(2):
                rows = slice(h * 256, (h + 1) * 256)
                down_ref[s, rows] = dot_nt(pick[rows], legendre_ref[s]).astype(BF)
                leaving[2 + 3 * s + h].start()

    return work, leaving


def ready_kernel(turn_ref, far_legendre, far_quad, _up, _down, _weight, *refs):
    far, buffers, results, sems = refs[:3], refs[3:5], refs[5:8], refs[8]

    @pl.when(turn_ref[0] == 1)
    def _():
        chosen = parted(buffers[0].shape[2])
        work, leaving = legendre_tables(chosen, (far_legendre, far_quad), buffers, results, far, sems)
        work()
        for copy in leaving:
            copy.wait()


def early_kernel(turn_ref, far_legendre, far_quad, far_order, far_table, *refs):
    far, far_early, buffers, results, sems = refs[:3], refs[3], refs[4:6], refs[6:9], refs[9]
    order_ref, table_ref, early_ref, more_sems = refs[10:]

    @pl.when(turn_ref[0] == 1)
    def _():
        chosen = parted(buffers[0].shape[2])
        work, leaving = legendre_tables(chosen, (far_legendre, far_quad), buffers, results, far, sems)
        coming = start_copies((far_order, far_table), (order_ref, table_ref), more_sems)
        work()
        coming[0].wait()
        orders = table_ref.shape[1]
        order = jnp.where(chosen, order_ref[...].astype(F32), 0.0)
        order = jnp.sum(order, axis=1, keepdims=True).astype(jnp.int32)
        scale = jnp.where(order == 0, 1.0, 2.0)
        placed = (iota((orders, orders), 1) == order).astype(BF)
        coming[1].wait()
        for r in range(2):
            early_ref[r] = (dot(placed, table_ref[r]) * (scale if r == 0 else -scale)).astype(BF)
            copy = pltpu.make_async_copy(early_ref.at[r], far_early.at[r], more_sems.at[2 + r])
            copy.start()
            leaving.append(copy)
        for copy in leaving:
            copy.wait()


def tall(row, count):
    block = jnp.broadcast_to(row, (16, row.shape[1])).astype(BF)
    return jnp.concatenate([block] * (count // 16), axis=0)


def synth_kernel(
    core_ref,
    slots_ref,
    next_ref,
    pre_ref,
    table_ref,
    early_ref,
    order_ref,
    sent_ref,
    grad_ref,
    slope_ref,
    rows_ref,
    cols_ref,
    field_ref,
    halves_ref,
    total_ref,
    msg_ref,
):
    values = pre_ref[...].astype(F32)
    cdf = 0.5 * (1.0 + lax.erf(values * 0.7071067811865476))
    density = jnp.exp(-0.5 * values * values) * 0.3989422804014327
    slope_ref[...] = cdf + values * density
    lat_dev, lons, width = next_ref.shape
    ranks = slots_ref.shape[0]
    capacity = 16
    groups = lons // 4
    orders = table_ref.shape[1]
    fields = slots_ref[...].T
    value = fields[0:16]
    lat_step = fields[16:32]
    lon_step = fields[32:48]
    corner = fields[48:64].astype(jnp.int32)
    chan = fields[64:80]
    group = (corner // 4).astype(F32)
    place = corner % 4
    at_left = ((1.0 - lat_step) * (1.0 - lon_step), lat_step * (1.0 - lon_step))
    at_right = ((1.0 - lat_step) * lon_step, lat_step * lon_step)
    weights = [
        jnp.where(place == j, at_left[k], 0.0) + jnp.where(place == j - 1, at_right[k], 0.0)
        for j in range(5)
        for k in range(lat_dev)
    ]
    chan_ids = iota((width, ranks), 0).astype(F32).astype(BF)
    group_ids = iota((groups, ranks), 0).astype(F32).astype(BF)
    nothing = jnp.zeros((), BF)
    for p in range(capacity):
        span = slice(p * ranks, (p + 1) * ranks)
        rows_ref[:, span] = jnp.where(
            group_ids == tall(group[p : p + 1], groups), tall(value[p : p + 1], groups), nothing
        )
        hit = chan_ids == tall(chan[p : p + 1], width)
        for i, weight in enumerate(weights):
            cols_ref[i * width : (i + 1) * width, span] = jnp.where(
                hit, tall(weight[p : p + 1], width), nothing
            )
    pair = lat_dev * width

    def found(j):
        return dot_nt(rows_ref[...], cols_ref[j * pair : (j + 1) * pair, :])

    for j in range(4):
        part = found(j)
        if j == 0:
            part = part + pltpu.roll(found(4), 1, 0)
        for k in range(lat_dev):
            field_ref[k, pl.ds(j, groups, stride=4), :] = part[:, k * width : (k + 1) * width]
    block = 128
    for k in range(lat_dev):
        for h in range(2):
            lanes = slice(h * pair + k * width, h * pair + (k + 1) * width)
            for i in range(lons // 2 // block):
                span = slice(h * lons // 2 + i * block, h * lons // 2 + (i + 1) * block)
                total = next_ref[k, span, :].astype(F32) + field_ref[k, span, :]
                grad_ref[k, span, :] = total
                halves_ref[i * block : (i + 1) * block, lanes] = (
                    total * slope_ref[k, span, :]
                ).astype(BF)

    def store(total, r):
        for s in range(2):
            for k in range(lat_dev):
                msg_ref[pl.ds(s * 4 + r * 2 + k, ranks, stride=8), :] = total[
                    s * ranks : (s + 1) * ranks, k * width : (k + 1) * width
                ]

    @pl.when(core_ref[0] == 0)
    def _():
        order = jnp.concatenate([order_ref[:, s : s + 1] for s in range(2)], axis=0)
        sign = jnp.where(order % 2 == 0, 1.0, -1.0)
        for r in range(2):
            both = dot(early_ref[r], halves_ref[...])
            store(both[:, :pair] + sign * both[:, pair:], r)

    @pl.when(core_ref[0] == 1)
    def _():
        chosen = [
            (iota((ranks, orders), 1) == order_ref[:, s : s + 1]).astype(BF) for s in range(2)
        ]
        chosen = jnp.concatenate(chosen, axis=0)
        order_ids = iota((orders, 1), 0)
        sign = jnp.where(order_ids % 2 == 0, 1.0, -1.0)
        scale = jnp.where(order_ids == 0, 1.0, 2.0)
        for r in range(2):
            both = dot(table_ref[r], halves_ref[...])
            total = (both[:, :pair] + sign * both[:, pair:]) * (scale if r == 0 else -scale)
            total_ref[:, r * pair : (r + 1) * pair] = total.astype(BF)
        for r in range(2):
            store(dot(chosen, total_ref[:, r * pair : (r + 1) * pair]), r)

    sent_ref[...] = msg_ref[...].reshape(ranks, 8, width).astype(BF)


def legendre_kernel(
    got_ref, up_ref, down_ref, weight_ref, saved_ref, gain_ref, first_ref, second_ref, msg_ref, out_ref, field_ref, coeff_ref
):
    ranks, rows, width = got_ref.shape
    msg_ref[...] = got_ref[...].astype(F32).reshape(ranks * rows, width)
    gain_real = gain_ref[0]
    gain_imag = gain_ref[1]
    terms = [None, None]
    for s in range(2):
        for r in range(2):
            for k in range(2):
                field_ref[s, k * ranks : (k + 1) * ranks, r * width : (r + 1) * width] = msg_ref[
                    pl.ds(s * 4 + r * 2 + k, ranks, stride=8), :
                ].astype(BF)
    for s in range(2):
        found = dot(up_ref[s], field_ref[s])
        real = found[:, :width]
        imag = found[:, width:]
        saved_real = saved_ref[s, 0].astype(F32)
        saved_imag = saved_ref[s, 1].astype(F32)
        coeff_ref[s, :, :width] = (gain_real * real + gain_imag * imag).astype(BF)
        coeff_ref[s, :, width:] = (gain_real * imag - gain_imag * real).astype(BF)
        new = (real * saved_real + imag * saved_imag, imag * saved_real - real * saved_imag)
        terms = [n if t is None else t + n for t, n in zip(terms, new)]
    for s in range(2):
        lat_grad = dot(down_ref[s], coeff_ref[s])
        for r in range(2):
            weighted = lat_grad[:, r * width : (r + 1) * width] * weight_ref[...]
            for k in range(2):
                out_ref[s, pl.ds(r * 2 + k, ranks, stride=8), :] = weighted[
                    k * ranks : (k + 1) * ranks
                ]
    for g in range(2):
        for h in range(2):
            part = terms[g][h * ranks : (h + 1) * ranks]
            for s in range(2):
                out_ref[s, pl.ds(4 + g * 2 + h, ranks, stride=8), :] = part
    first_ref[...] = out_ref[0].reshape(ranks, rows, width).astype(BF)
    second_ref[...] = out_ref[1].reshape(ranks, rows, width).astype(BF)


def share_kernel(got_ref, half_ref, sent_ref):
    ranks, rows, width = got_ref.shape
    part = ranks // 16
    total = got_ref[0:part].astype(F32)
    for i in range(1, 16):
        total = total + got_ref[i * part : (i + 1) * part].astype(F32)
    total = jnp.sum(total, axis=0, keepdims=True).astype(BF)
    sent_ref[...] = jnp.where(iota(got_ref.shape, 1) < 4, half_ref[...], total)


def field_kernel(
    first_ref, second_ref, order_ref, table_ref, grad_ref, out_ref, gain_ref, msg_ref, field_ref, share_ref, sems
):
    lat_dev, lons, width = grad_ref.shape
    ranks = first_ref.shape[0]
    half = lons // 2
    msg_ref[1] = second_ref[...].astype(F32).reshape(msg_ref.shape[1:])
    for g in range(2):
        for h in range(2):
            share_ref[g, h * ranks : (h + 1) * ranks, :] = msg_ref[
                1, pl.ds(4 + g * 2 + h, ranks, stride=8), :
            ]
    copies = [pltpu.make_async_copy(share_ref, gain_ref, sems.at[0])]
    copies[0].start()
    msg_ref[0] = first_ref[...].astype(F32).reshape(msg_ref.shape[1:])
    row = iota((half, ranks), 0)
    order = (row % ranks) * 2 + row // ranks
    chosen = [(order == order_ref[s : s + 1, :]).astype(BF) for s in range(2)]
    chosen = jnp.concatenate(chosen, axis=1)
    placed = []
    for r in range(2):
        parts = []
        for s in range(2):
            lanes = [msg_ref[s, pl.ds(r * 2 + k, ranks, stride=8), :].astype(BF) for k in range(2)]
            parts.append(jnp.concatenate(lanes, axis=1))
        placed.append(dot(chosen, jnp.concatenate(parts, axis=0)).astype(BF))
    even = jnp.concatenate([p[:ranks] for p in placed], axis=0)
    odd = jnp.concatenate([p[ranks:] for p in placed], axis=0)
    block = half // 4
    for i in range(4):
        rows = slice(i * block, (i + 1) * block)
        same = dot(table_ref[0, rows, :], even)
        turned = dot(table_ref[1, rows, :], odd)
        for h in range(2):
            span = slice(h * half + i * block, h * half + (i + 1) * block)
            for k in range(lat_dev):
                lanes = slice(k * width, (k + 1) * width)
                part = same[:, lanes] + turned[:, lanes] if h == 0 else same[:, lanes] - turned[:, lanes]
                field_ref[k, span, :] = (grad_ref[k, span, :] + part).astype(BF)
            copies.append(
                pltpu.make_async_copy(
                    field_ref.at[:, span, :], out_ref.at[:, span, :], sems.at[len(copies)]
                )
            )
            copies[-1].start()
    for copy in copies:
        copy.wait()


def exchange(message):
    return lax.all_to_all(message, RANKS, split_axis=0, concat_axis=0, tiled=True)


def on_device(
    next_grad,
    pre_act,
    legendre,
    order_slots,
    quad_weights,
    spectral_gain,
    saved_coeffs,
    obs_value,
    obs_lat_frac,
    obs_lon_frac,
    obs_corner,
    obs_channel,
    slot_counts,
):
    lat_dev, lons, width = next_grad.shape
    slot_dev, degrees, lats = legendre.shape
    orders = order_slots.shape[0]
    ranks = lax.axis_size("lat") * lax.axis_size("obs")
    shape = jax.ShapeDtypeStruct

    index = np.arange(orders)
    angle = ((index[:, None] * index[None, :]) % lons).astype(np.float32) * np.float32(
        2.0 * math.pi / lons
    )
    waves = np.stack([np.cos(angle), np.sin(angle)]).astype(jnp.bfloat16)
    table = jnp.asarray(waves)
    back = np.stack([waves[0].astype(np.float32), -waves[1].astype(np.float32)]) / lons
    back = [np.concatenate([back[0, :, p::2], back[1, :, p::2]], axis=1) for p in range(2)]
    back = jnp.asarray(np.stack(back).astype(jnp.bfloat16))

    core = lax.axis_index("chan").astype(jnp.int32).reshape(1)
    slot_args = (
        obs_value[0],
        obs_lat_frac[0],
        obs_lon_frac[0],
        obs_corner[0],
        obs_channel[0],
        slot_counts,
    )
    packed = call(
        pack_kernel,
        shape((ranks, 128), F32),
        scratch=buffers_for(slot_args),
        smem=1,
        far=range(1, 7),
        limit=60,
    )(core * width, *slot_args)

    ready_args = (legendre, quad_weights.reshape(1, lats))
    ready = (
        shape(legendre.shape, BF),
        shape((slot_dev, lats, degrees), BF),
        shape((lats, 128), F32),
    )
    ready_scratch = (
        buffers_for(ready_args)[:-1] + buffers_for(ready)[:-1] + [pltpu.SemaphoreType.DMA((10,))]
    )
    early_args = (order_slots.reshape(1, orders), table)

    *prepared, early = call(
        early_kernel,
        (*ready, shape(table.shape, BF)),
        scratch=ready_scratch
        + buffers_for(early_args)[:-1]
        + [pltpu.VMEM(table.shape, BF), pltpu.SemaphoreType.DMA((4,))],
        smem=1,
        far=range(1, 5),
        far_out=True,
        flops=6 * 2 * 512**3,
        limit=60,
    )(1 - core, *ready_args, *early_args)
    packed, prepared, early = lax.optimization_barrier((packed, prepared, early))
    slots = exchange(packed)
    prepared = call(
        ready_kernel,
        ready,
        scratch=ready_scratch,
        smem=1,
        far=range(1, 6),
        far_out=True,
        aliases={3: 0, 4: 1, 5: 2},
        flops=4 * 2 * 512**3,
        limit=60,
    )(core, *ready_args, *prepared)
    order_columns = order_slots.reshape(ranks, 2)
    slots, prepared, order_columns, order_rows = lax.optimization_barrier(
        (slots, prepared, order_columns, order_columns.T)
    )
    up_table, down_table, weight = prepared

    message = shape((ranks, 8, width), BF)
    rows = pltpu.VMEM((ranks * 8, width), F32)
    pairs = pltpu.VMEM((2, ranks * 8, width), F32)
    field = shape(next_grad.shape, F32)
    sent, out_grad = call(
        synth_kernel,
        (message, field),
        scratch=[
            pltpu.VMEM(field.shape, F32),
            pltpu.VMEM((lons // 4, 16 * ranks), BF),
            pltpu.VMEM((10 * width, 16 * ranks), BF),
            pltpu.VMEM(field.shape, F32),
            pltpu.VMEM((lons // 2, 2 * lat_dev * width), BF),
            pltpu.VMEM((orders, 2 * lat_dev * width), BF),
            rows,
        ],
        smem=1,
        flops=2 * 1024 * 4096 * 512,
        limit=32,
    )(core, slots, next_grad, pre_act, table, early, order_columns)
    by_order = exchange(sent)
    first, second = call(
        legendre_kernel,
        (message, message),
        scratch=[rows, pairs]
        + [pltpu.VMEM((slot_dev, n, 2 * width), BF) for n in (lats, degrees)],
        flops=2 * 512**3 * 4
    )(by_order, up_table, down_table, weight, saved_coeffs, spectral_gain)
    first = exchange(first)
    second = exchange(call(share_kernel, message)(first, second))
    outs = (shape(next_grad.shape, BF), shape((2, degrees, width), F32))
    return call(
        field_kernel,
        outs,
        scratch=[pairs]
        + [pltpu.VMEM(o.shape, o.dtype) for o in outs]
        + [pltpu.SemaphoreType.DMA((9,))],
        far_out=True,
        flops=2 * 512**3 * 3,
    )(first, second, order_rows, back, out_grad)


def solution(mesh):
    ranks = P(RANKS, None, None)
    in_specs = (
        P(RANKS, None, "chan"),
        P(RANKS, None, "chan"),
        ranks,
        P(),
        P(),
        P(None, None, "chan"),
        P(RANKS, None, None, "chan"),
        ranks,
        ranks,
        ranks,
        ranks,
        ranks,
        P(RANKS, None),
    )
    out_specs = (P(RANKS, None, "chan"), P(None, None, "chan"))
    return jax.shard_map(
        on_device, mesh=mesh, in_specs=in_specs, out_specs=out_specs, check_vma=False
    )
```
